256 devices in a mesh: row: 8 (over y_lo, x), col: 16 (over z, y_hi), layer: 2 (over core).
Axes of the slice: x: 4, y: 4 (y_hi: 2, y_lo: 2; y = y_hi * 2 + y_lo), z: 8, core: 2. Of those that a mesh axis runs over, the one named last changes fastest.
Arguments:
- initial: float32 [4096, 4096], P('row', 'col'), may hold values from -1.1 to 1.1
- pattern: int32 [32, 32], P('row', 'col'), may hold values from 0 to 1
- filters: int32 [2, 32, 32], P(None, 'row', 'col'), may hold values 0 or 1
Outputs:
- sign_matrix: float32 [4096, 4096], P('row', ('col', 'layer'))
The draws below stay inside these ranges and needn't reach their ends.
All inputs are finite; a program needn't handle non-finite values. No bound on the sum of `filters` on one device may be relied on, other than what follows from the above.
Results may differ from the reference program's by a relative error of at most 0.00012.
Values sent between devices are 32-bit elements; how exact they have to be, the bound alone decides.
A program may use at most 64 MiB of HBM per device.

```python
import jax
import jax.numpy as jnp
from jax import lax

TILE = 128
ITERS = 2
NT = 32


def draw_initial(key, part):
    key = jax.random.fold_in(key, 11)
    noise_key, size_key, sign_key = jax.random.split(key, 3)
    order_total = NT * TILE
    spread = 0.2 * (2.0 / order_total) ** 0.5
    noise = jnp.clip(jax.random.normal(noise_key, (order_total, order_total), jnp.float32), -5.0, 5.0)
    magnitude = jax.random.uniform(size_key, (order_total,), jnp.float32, 0.3, 0.9)
    signs = jnp.where(jax.random.bernoulli(sign_key, 0.5, (order_total,)), 1.0, -1.0).astype(jnp.float32)
    return noise * spread + jnp.diag(signs * magnitude)


def draw_pattern(key, part):
    key = jax.random.fold_in(key, 12)
    band_key, extra_key = jax.random.split(key)
    band = jax.random.randint(band_key, (NT,), 1, NT // 2 + 1)
    extra = jax.random.randint(extra_key, (NT, NT), 0, 4)
    row_ids = jnp.arange(NT, dtype=jnp.int32)[:, None]
    col_ids = jnp.arange(NT, dtype=jnp.int32)[None, :]
    apart = jnp.abs(row_ids - col_ids)
    circular = jnp.minimum(apart, NT - apart)
    kept = (circular <= band[:, None]) | (extra == 0)
    return kept.astype(jnp.int32)


def plant(drawn, stream_key, low, top_value):
    longest = drawn.shape.index(max(drawn.shape))
    spots = []
    for shift in (0, 1):
        where = [jax.random.randint(jax.random.fold_in(stream_key, axis), (), 0, length) for axis, length in enumerate(drawn.shape)]
        where[longest] = (where[longest] + shift) % drawn.shape[longest]
        spots.append(tuple(where))
    return drawn.at[spots[0]].set(low).at[spots[1]].set(top_value)


def setup_inputs(seed: int = 0) -> dict:
    streams_of = jax.random.split(jax.random.key(seed), 4)
    return {
        "initial": draw_initial(jax.random.fold_in(streams_of[3], 71), 0),
        "pattern": draw_pattern(jax.random.fold_in(streams_of[3], 71), 0),
        "filters": plant((jax.random.randint(streams_of[2], (ITERS, NT, NT), 0, 4) < 3).astype(jnp.int32), jax.random.fold_in(streams_of[2], 1), 0, 1),
    }


def expand_tiles(tiles):
    values = tiles.astype(jnp.float32)
    row_tiles, col_tiles = values.shape
    spread = jnp.broadcast_to(values[:, None, :, None], (row_tiles, TILE, col_tiles, TILE))
    return spread.reshape(row_tiles * TILE, col_tiles * TILE)


def reference(initial, pattern, filters):
    matrix = initial * expand_tiles(pattern)
    for sweep in range(ITERS):
        filter_mask = expand_tiles(filters[sweep])
        square = filter_mask * jnp.dot(matrix, matrix, precision=lax.Precision.HIGHEST, preferred_element_type=jnp.float32)
        product = jnp.dot(matrix, square, precision=lax.Precision.HIGHEST, preferred_element_type=jnp.float32)
        matrix = 1.5 * matrix - 0.5 * filter_mask * product
    return matrix
```

```python
import jax
import jax.numpy as jnp
from jax import lax
from jax.experimental import pallas as pl
from jax.experimental.pallas import tpu as pltpu
from jax.sharding import PartitionSpec as P

MESH = pl.DeviceIdType.MESH
TILE = 128
ITERS = 2
F32 = jnp.float32
BF16 = jnp.bfloat16
ORDER = (0, 2, 1, 3)


def halves(value):
    high = value.astype(BF16)
    return high, (value - high.astype(F32)).astype(BF16)


def dot3(a_high, a_low, b_high, b_low):
    def dot(a, b):
        return jnp.dot(a, b, preferred_element_type=F32)

    return dot(a_high, b_high) + (dot(a_high, b_low) + dot(a_low, b_high))


def kernel(
    initial, pattern, filters, out,
    own, a_in, b_in, s_in, a_hi, a_lo, b_hi, b_lo, s_hi, s_lo, sq_part, sq_from, pr_part, pr_from,
    a_send, a_recv, y_send, y_recv, g_send, g_recv, e_send, e_recv,
):
    row, col, layer = lax.axis_index("row"), lax.axis_index("col"), lax.axis_index("layer")
    x, y_lo = lax.rem(row, 4), row // 4
    z, y_hi = col // 2, lax.rem(col, 2)
    native = y_hi == layer

    def at_x(step):
        return {"row": y_lo * 4 + lax.rem(x + step + 4, 4)}

    def at_z(step):
        return {"col": lax.rem(z + step + 8, 8) * 2 + y_hi}

    mate_lo = {"row": (1 - y_lo) * 4 + x}
    mate_hi = {"col": z * 2 + (1 - y_hi)}
    sibling = {"layer": 1 - layer}

    barrier = pltpu.get_barrier_semaphore()
    neighbours = (at_x(1), at_x(-1), at_z(1), at_z(-1), mate_lo, mate_hi, sibling)
    for device in neighbours:
        pl.semaphore_signal(barrier, inc=1, device_id=device, device_id_type=MESH)

    def tile_mask(ref, index, value):
        parts = []
        for ct in range(2):
            parts.append(value[:, ct * TILE : (ct + 1) * TILE] * ref[(*index, ct)].astype(F32))
        return jnp.concatenate(parts, axis=1)

    def rows_of(tile):
        return pl.ds(tile * TILE, TILE)

    def remote(src, dst, send, recv, device):
        return pltpu.make_async_remote_copy(
            src_ref=src, dst_ref=dst, send_sem=send, recv_sem=recv, device_id=device, device_id_type=MESH
        )

    def z_copy(it, k, way, depth):
        slot = lax.rem(z - depth + 8, 8) if way == 0 else lax.rem(z + depth, 8)
        piece = a_in.at[it, slot, rows_of(ORDER[k]), :]
        return remote(piece, piece, a_send.at[it, k, way, depth], a_recv.at[it, k, way, depth], at_z(1 if way == 0 else -1))

    def y_copy(it, k):
        piece = a_in.at[it, z, rows_of(ORDER[k]), :]
        return remote(piece, piece, y_send.at[it, k], y_recv.at[it, k], mate_hi)

    def split_a(it, k, slot):
        for part in range(2):
            high, low = halves(a_in[it, slot, rows_of(ORDER[k]), part * TILE : (part + 1) * TILE])
            columns = pl.ds(pl.multiple_of(part * 1024 + slot * TILE, TILE), TILE)
            a_hi[k * TILE : (k + 1) * TILE, columns] = high
            a_lo[k * TILE : (k + 1) * TILE, columns] = low

    def split_b(src, high_ref, low_ref, it, part, slot):
        high, low = halves(src[it, slot, part])
        rows = pl.ds(pl.multiple_of(part * 1024 + slot * TILE, TILE), TILE)
        high_ref[rows, :] = high
        low_ref[rows, :] = low

    class Gather:
        def __init__(self, buf, it, kind, part, finish):
            self.buf, self.it, self.part, self.finish = buf, it, part, finish
            self.base = (it, kind, part)
            self.sent = []

        def copy(self, index, slot, device, half=None):
            piece = self.buf.at[self.it, slot, self.part]
            if half is not None:
                piece = self.buf.at[self.it, slot, self.part, pl.ds(half * 64, 64), :]
            return remote(piece, piece, g_send.at[(*self.base, index)], g_recv.at[(*self.base, index)], device)

        def start(self, copy):
            copy.start()
            self.sent.append(copy)
            return copy

        def slot(self, group, step):
            lane = y_lo if group == 0 else 1 - y_lo
            return lane * 4 + lax.rem(x + step + 4, 4)

        def begin(self):
            self.mate = self.start(self.copy(0, self.slot(0, 0), mate_lo))
            self.spread(0)

        def spread(self, group):
            first = 1 + group * 4
            right = self.start(self.copy(first, self.slot(group, 0), at_x(1)))
            left = self.start(self.copy(first + 1, self.slot(group, 0), at_x(-1)))
            if group == 0:
                self.near = [(right, left)]
            else:
                self.near.append((right, left))

        def from_mate(self):
            self.mate.wait_recv()
            self.spread(1)
            self.finish(self.slot(1, 0))

        def from_near(self, group):
            right, left = self.near[group]
            first = 1 + group * 4
            right.wait_recv()
            far_right = self.start(self.copy(first + 2, self.slot(group, -1), at_x(1), 0))
            self.finish(self.slot(group, -1))
            left.wait_recv()
            far_left = self.start(self.copy(first + 3, self.slot(group, 1), at_x(-1), 1))
            self.finish(self.slot(group, 1))
            if group == 0:
                self.far = [(far_right, far_left)]
            else:
                self.far.append((far_right, far_left))

        def from_far(self, group):
            for copy in self.far[group]:
                copy.wait_recv()
            self.finish(self.slot(group, 2))

        def drain(self):
            for copy in self.sent:
                copy.wait_send()

    def load_tiles(it, part):
        @pl.when(native)
        def _():
            for tile in (part, 2 + part):
                a_in[it, z, rows_of(tile), :] = own[rows_of(tile), :]
                y_copy(it, ORDER.index(tile)).start()

        mine = pl.ds(pl.multiple_of((2 * layer + part) * TILE, TILE), TILE)
        b_in[it, row, part] = own[mine, :]

    for tile in range(4):
        own[rows_of(tile), :] = tile_mask(pattern, (tile,), initial[rows_of(tile), :])
    pl.semaphore_wait(barrier, len(neighbours))

    for it in range(ITERS):
        z_sent = []

        def z_start(k, way, depth):
            copy = z_copy(it, k, way, depth)
            copy.start()
            z_sent.append(copy)

        def z_begin(k):
            if k < 4:
                @pl.when(jnp.logical_not(native))
                def _():
                    y_copy(it, k).wait_recv()

                z_start(k, 0, 0)
                z_start(k, 1, 0)
                split_a(it, k, z)

        def z_step(k, depth):
            for way in range(2):
                if depth == 4 and way != k % 2:
                    continue
                z_copy(it, k, way, depth - 1).wait_recv()
                if depth < 3 or (depth == 3 and way == k % 2):
                    z_start(k, way, depth)
                slot = lax.rem(z - depth + 8, 8) if way == 0 else lax.rem(z + depth, 8)
                split_a(it, k, slot)

        gathers = []

        def gather(buf, kind, part, high_ref, low_ref):
            g = Gather(buf, it, kind, part, lambda slot: split_b(buf, high_ref, low_ref, it, part, slot))
            gathers.append(g)
            return g

        def square(part):
            rows = slice(part * 256, (part + 1) * 256)
            value = dot3(a_hi[rows, :], a_lo[rows, :], b_hi[...], b_lo[...])
            sq_part[it, part, 0] = value[:TILE]
            sq_part[it, part, 1] = value[TILE:]
            copy = remote(
                sq_part.at[it, part, 1 - layer], sq_from.at[it, part],
                e_send.at[it, part], e_recv.at[it, part], sibling,
            )
            copy.start()
            return copy

        def square_ready(part, copy):
            copy.wait_recv()
            value = sq_part[it, part, layer] + sq_from[it, part]
            s_in[it, row, part] = tile_mask(filters, (it, 2 * layer + part), value)
            g = gather(s_in, 1, part, s_hi, s_lo)
            g.begin()
            split_b(s_in, s_hi, s_lo, it, part, row)
            return g

        b0 = gather(b_in, 0, 0, b_hi, b_lo)
        b1 = gather(b_in, 0, 1, b_hi, b_lo)
        load_tiles(it, 0)
        b0.begin()
        load_tiles(it, 1)
        b1.begin()
        split_b(b_in, b_hi, b_lo, it, 0, row)
        split_b(b_in, b_hi, b_lo, it, 1, row)
        z_begin(0)
        z_begin(1)
        b0.from_mate()
        b1.from_mate()
        z_step(0, 1)
        b0.from_near(0)
        z_step(1, 1)
        b1.from_near(0)
        z_step(0, 2)
        b0.from_near(1)
        z_step(1, 2)
        b1.from_near(1)
        z_step(0, 3)
        b0.from_far(0)
        b1.from_far(0)
        z_step(1, 3)
        z_begin(2)
        z_begin(3)
        b0.from_far(1)
        b1.from_far(1)
        z_step(0, 4)
        z_step(1, 4)
        half = square(0)
        z_step(2, 1)
        s0 = square_ready(0, half)
        z_step(3, 1)
        s0.from_mate()
        z_step(2, 2)
        s0.from_near(0)
        z_step(3, 2)
        s0.from_near(1)
        z_step(2, 3)
        s0.from_far(0)
        z_step(3, 3)
        s0.from_far(1)
        z_step(2, 4)
        z_step(3, 4)
        half = square(1)
        s1 = square_ready(1, half)
        s1.from_mate()
        for part in range(2):
            rows = slice(part * 256, (part + 1) * 256)
            pr_part[it, rows, :] = dot3(
                a_hi[rows, :1024], a_lo[rows, :1024], s_hi[:1024, :], s_lo[:1024, :]
            )
        s1.from_near(0)
        s1.from_near(1)
        s1.from_far(0)
        s1.from_far(1)
        copies = []
        for part in range(2):
            rows = slice(part * 256, (part + 1) * 256)
            pr_part[it, rows, :] += dot3(
                a_hi[rows, 1024:], a_lo[rows, 1024:], s_hi[1024:, :], s_lo[1024:, :]
            )
            copy = remote(
                pr_part.at[it, pl.ds(part * 256, 256), :], pr_from.at[it, pl.ds(part * 256, 256), :],
                e_send.at[it, 2 + part], e_recv.at[it, 2 + part], sibling,
            )
            copy.start()
            copies.append(copy)
        for part in range(2):
            copies[part].wait_recv()
            for k in (2 * part, 2 * part + 1):
                tile = ORDER[k]
                rows = slice(k * TILE, (k + 1) * TILE)
                value = tile_mask(filters, (it, tile), pr_part[it, rows, :] + pr_from[it, rows, :])
                own[rows_of(tile), :] = 1.5 * own[rows_of(tile), :] - 0.5 * value

        for copy in z_sent:
            copy.wait_send()
        for g in gathers:
            g.drain()
        for index in range(2):
            remote(
                sq_part.at[it, index, 1 - layer], sq_from.at[it, index],
                e_send.at[it, index], e_recv.at[it, index], sibling,
            ).wait_send()
        for copy in copies:
            copy.wait_send()

        @pl.when(native)
        def _():
            for k in range(4):
                y_copy(it, k).wait_send()

    out[...] = own[:, pl.ds(pl.multiple_of(layer * TILE, TILE), TILE)]


def on_device(initial, pattern, filters):
    dma = pltpu.SemaphoreType.DMA
    vmem = pltpu.VMEM
    return pl.pallas_call(
        kernel,
        out_shape=jax.ShapeDtypeStruct((512, TILE), F32),
        in_specs=[
            pl.BlockSpec(memory_space=pltpu.VMEM),
            pl.BlockSpec(memory_space=pltpu.SMEM),
            pl.BlockSpec(memory_space=pltpu.SMEM),
        ],
        out_specs=pl.BlockSpec(memory_space=pltpu.VMEM),
        scratch_shapes=[
            vmem((512, 256), F32),
            vmem((ITERS, 8, 512, 256), F32),
            vmem((ITERS, 8, 2, TILE, 256), F32),
            vmem((ITERS, 8, 2, TILE, 256), F32),
            vmem((512, 2048), BF16),
            vmem((512, 2048), BF16),
            vmem((2048, 256), BF16),
            vmem((2048, 256), BF16),
            vmem((2048, 256), BF16),
            vmem((2048, 256), BF16),
            vmem((ITERS, 2, 2, TILE, 256), F32),
            vmem((ITERS, 2, TILE, 256), F32),
            vmem((ITERS, 512, 256), F32),
            vmem((ITERS, 512, 256), F32),
            dma((ITERS, 4, 2, 4)),
            dma((ITERS, 4, 2, 4)),
            dma((ITERS, 4)),
            dma((ITERS, 4)),
            dma((ITERS, 2, 2, 9)),
            dma((ITERS, 2, 2, 9)),
            dma((ITERS, 4)),
            dma((ITERS, 4)),
        ],
        compiler_params=pltpu.CompilerParams(
            collective_id=0, has_side_effects=True, vmem_limit_bytes=52 << 20
        ),
        name="sign_iterations",
    )(initial, pattern, filters)


def solution(mesh):
    return jax.shard_map(
        on_device,
        mesh=mesh,
        in_specs=(P("row", "col"), P("row", "col"), P(None, "row", "col")),
        out_specs=P("row", ("col", "layer")),
        check_vma=False,
    )
```

```python
import jax
import jax.numpy as jnp
from jax import lax
from jax.experimental import pallas as pl
from jax.experimental.pallas import tpu as pltpu
from jax.sharding import PartitionSpec as P

MESH = pl.DeviceIdType.MESH
TILE = 128
ITERS = 2
PARTS = 4
DEPTH = 64
F32 = jnp.float32
BF16 = jnp.bfloat16
BY_PARTNER = (1, 3)
FAR_BY_MATE = False
STRAIGHT = (3,)
STEPS = [
    ("bg", 0), ("zb", 2), ("y", 1), ("zb", 3), ("zb", 0), ("y", 0), ("gn", "B", 0, 0), ("bg", 1), ("zb", 1),
    ("gm", "B", 0), ("y", 2), ("bg", 3), ("yb", 0), ("gm", "B", 1), ("z", 0, 0, 1), ("bg", 2), ("gf", "B", 0, 0),
    ("yb", 1), ("z", 0, 1, 1), ("gm", "B", 3), ("z", 1, 0, 1), ("gn", "B", 1, 0), ("z", 0, 0, 2),
    ("gn", "B", 3, 0), ("gm", "B", 2), ("z", 0, 1, 2), ("gn", "B", 0, 1), ("y", 3), ("z", 1, 0, 2), ("z", 0, 2, 1),
    ("gn", "B", 2, 0), ("gn", "B", 3, 1), ("z", 1, 1, 1), ("gn", "B", 1, 1), ("yb", 2), ("z", 0, 1, 3),
    ("z", 0, 0, 3), ("gn", "B", 2, 1), ("gf", "B", 1, 0), ("gf", "B", 3, 0), ("z", 1, 0, 3), ("z", 1, 1, 2),
    ("z", 0, 3, 1), ("gf", "B", 2, 0), ("yb", 3), ("gf", "B", 3, 1), ("gf", "B", 1, 1), ("z", 1, 2, 1),
    ("z", 0, 1, 4), ("z", 0, 0, 4), ("gf", "B", 2, 1), ("gf", "B", 0, 1), ("z", 0, 2, 2), ("z", 1, 0, 4),
    ("sq", 0), ("z", 0, 3, 2), ("z", 1, 1, 3), ("z", 1, 2, 2), ("sr", 0), ("z", 1, 1, 4), ("sq", 1),
    ("z", 0, 2, 3), ("sr", 1), ("z", 1, 2, 3), ("z", 1, 3, 1), ("z", 1, 3, 2), ("z", 0, 3, 3), ("gm", "S", 0),
    ("z", 0, 2, 4), ("gm", "S", 1), ("z", 1, 2, 4), ("sq", 2), ("z", 0, 3, 4), ("gn", "S", 0, 0),
    ("gn", "S", 0, 1), ("sr", 2), ("z", 1, 3, 3), ("gn", "S", 1, 0), ("gn", "S", 1, 1), ("z", 1, 3, 4), ("sq", 3),
    ("gm", "S", 2), ("gf", "S", 0, 0), ("sr", 3), ("gf", "S", 1, 1), ("gn", "S", 2, 1), ("gf", "S", 0, 1),
    ("gf", "S", 1, 0), ("gn", "S", 2, 0), ("pr0", 1), ("gd", "S", 3, 0), ("pr0", 0), ("gf", "S", 2, 0),
    ("gf", "S", 2, 1), ("gd", "S", 3, 1),
]


def halves(value):
    high = value.astype(BF16)
    return high, (value - high.astype(F32)).astype(BF16)


def dot3(a_high, a_low, b_high, b_low):
    def dot(a, b):
        return jnp.dot(a, b, preferred_element_type=F32)

    return dot(a_high, b_high) + (dot(a_high, b_low) + dot(a_low, b_high))


def kernel(
    initial, pattern, filters, out,
    own, a_in, b_in, s_in, a_hi, a_lo, b_hi, b_lo, s_hi, s_lo, sq_part, sq_from, pr_part, pr_from,
    a_send, a_recv, y_send, y_recv, p_send, p_recv, g_send, g_recv, e_send, e_recv,
):
    row, col, layer = lax.axis_index("row"), lax.axis_index("col"), lax.axis_index("layer")
    x, y_lo = lax.rem(row, 4), row // 4
    z, y_hi = col // 2, lax.rem(col, 2)
    def at_x(step):
        return {"row": y_lo * 4 + lax.rem(x + step + 4, 4)}

    def at_z(step):
        return {"col": lax.rem(z + step + 8, 8) * 2 + y_hi}

    def mate_x(step):
        return {"row": (1 - y_lo) * 4 + lax.rem(x + step + 4, 4)}

    mate_lo = mate_x(0)
    mate_hi = {"col": z * 2 + (1 - y_hi)}
    sibling = {"layer": 1 - layer}

    barrier = pltpu.get_barrier_semaphore()
    neighbours = (at_x(1), at_x(-1), at_z(1), at_z(-1), mate_lo, mate_hi, sibling)
    if STRAIGHT:
        neighbours += (at_x(2), mate_x(1), mate_x(-1), mate_x(2))
    for device in neighbours:
        pl.semaphore_signal(barrier, inc=1, device_id=device, device_id_type=MESH)

    def tile_mask(ref, index, value):
        parts = []
        for ct in range(2):
            parts.append(value[:, ct * TILE : (ct + 1) * TILE] * ref[(*index, ct)].astype(F32))
        return jnp.concatenate(parts, axis=1)

    def remote(src, dst, send, recv, device):
        return pltpu.make_async_remote_copy(
            src_ref=src, dst_ref=dst, send_sem=send, recv_sem=recv, device_id=device, device_id_type=MESH
        )

    def z_slot(group, way, depth):
        at = lax.rem(z - depth + 8, 8) if way == 0 else lax.rem(z + depth, 8)
        return 2 * at + (y_hi if group == 0 else 1 - y_hi)

    def far_way(group, k):
        return k % 2 if k in BY_PARTNER else (k + group) % 2

    def a_piece(it, k, slot):
        return a_in.at[it, slot, k // 2, :, k % 2]

    def z_copy(it, group, k, way, depth):
        piece = a_piece(it, k, z_slot(group, way, depth))
        place = (it, group, k, way, depth)
        return remote(piece, piece, a_send.at[place], a_recv.at[place], at_z(1 - 2 * way))

    def y_copy(it, k):
        piece = a_piece(it, k, col)
        return remote(piece, piece, y_send.at[it, k], y_recv.at[it, k], mate_hi)

    def p_copy(it, k, way, depth):
        piece = a_piece(it, k, z_slot(0, way, depth))
        place = (it, BY_PARTNER.index(k), way, depth - 1)
        return remote(piece, piece, p_send.at[place], p_recv.at[place], mate_hi)

    def split_a(it, k, slot):
        columns = pl.ds(pl.multiple_of(lax.rem(slot, 2) * 1024 + slot // 2 * TILE, TILE), TILE)
        for side in range(2):
            rows = slice((2 * k + side) * DEPTH, (2 * k + side + 1) * DEPTH)
            high, low = halves(a_in[it, slot, k // 2, side, k % 2])
            a_hi[rows, columns] = high
            a_lo[rows, columns] = low

    bufs = {"B": (b_in, b_hi, b_lo), "S": (s_in, s_hi, s_lo)}

    def split_b(it, kind, part, slot):
        buf, high_ref, low_ref = bufs[kind]
        high, low = halves(buf[it, slot, part])
        rows = pl.ds(pl.multiple_of(part // 2 * 1024 + slot * TILE + part % 2 * DEPTH, DEPTH), DEPTH)
        high_ref[rows, :] = high
        low_ref[rows, :] = low

    def g_slot(group, step):
        lane = y_lo if group == 0 else 1 - y_lo
        return lane * 4 + lax.rem(x + step + 4, 4)

    def g_copy(it, kind, part, what):
        way = (part + what - 5) % 2
        if kind == "S" and part in STRAIGHT:
            slot = row
            device = (mate_lo, at_x(1), at_x(-1), mate_x(1), mate_x(-1), at_x(2), mate_x(2))[what]
        elif what == 0:
            slot, device = g_slot(0, 0), mate_lo
        elif what < 5:
            slot, device = g_slot((what - 1) // 2, 0), at_x(1 if what % 2 else -1)
        elif what == 6 and FAR_BY_MATE:
            slot, device = g_slot(0, 2), mate_lo
        else:
            slot, device = g_slot(what - 5, 2 * way - 1), at_x(1 - 2 * way)
        piece = bufs[kind][0].at[it, slot, part]
        place = (it, "BS".index(kind), part, what)
        return remote(piece, piece, g_send.at[place], g_recv.at[place], device)

    def e_copy(it, part):
        return remote(
            sq_part.at[it, part, 1 - layer], sq_from.at[it, part], e_send.at[it, part], e_recv.at[it, part], sibling
        )

    def pr_copy(it, part):
        rows = pl.ds(part * 256, 256)
        columns = slice(None)
        if it == ITERS - 1:
            columns = pl.ds(pl.multiple_of((1 - layer) * TILE, TILE), TILE)
        return remote(
            pr_part.at[it, rows, columns], pr_from.at[it, rows, columns],
            e_send.at[it, PARTS + part], e_recv.at[it, PARTS + part], sibling,
        )

    mine = pl.ds(pl.multiple_of(layer * TILE, TILE), TILE)

    def own_part(it, part):
        a_in[it, col, part // 2, :, part % 2] = own[part // 2, :, part % 2, :, mine]
        split_a(it, part, col)
        b_in[it, row, part] = own[part // 2, layer, part % 2]
        split_b(it, "B", part, row)

    def iteration(it):
        def y_begin(k):
            y_copy(it, k).start()

        def z_begin(k):
            z_copy(it, 0, k, 0, 0).start()
            z_copy(it, 0, k, 1, 0).start()

        def y_arrives(k):
            y_copy(it, k).wait_recv()
            if k not in BY_PARTNER:
                z_copy(it, 1, k, 0, 0).start()
                z_copy(it, 1, k, 1, 0).start()
            split_a(it, k, z_slot(1, 0, 0))

        def z_arrives(group, k, depth):
            for way in range(2):
                if depth == 4 and way != far_way(group, k):
                    continue
                if group == 1 and k in BY_PARTNER:
                    p_copy(it, k, way, depth).wait_recv()
                else:
                    z_copy(it, group, k, way, depth - 1).wait_recv()
                    if depth < 3 or (depth == 3 and way == far_way(group, k)):
                        z_copy(it, group, k, way, depth).start()
                    if k in BY_PARTNER:
                        p_copy(it, k, way, depth).start()
                split_a(it, k, z_slot(group, way, depth))

        def column_begin(part):
            for what in range(3):
                g_copy(it, "B", part, what).start()

        def straight(kind, part, far):
            for what in (3, 4, 5, 6) if far else (0, 1, 2):
                g_copy(it, kind, part, what).wait_recv()
                slot = (
                    g_slot(1, 0), g_slot(0, -1), g_slot(0, 1), g_slot(1, -1), g_slot(1, 1), g_slot(0, 2), g_slot(1, 2)
                )[what]
                split_b(it, kind, part, slot)

        def from_mate(kind, part):
            g_copy(it, kind, part, 0).wait_recv()
            g_copy(it, kind, part, 3).start()
            g_copy(it, kind, part, 4).start()
            split_b(it, kind, part, g_slot(1, 0))

        def from_near(kind, part, group):
            for way in range(2):
                g_copy(it, kind, part, 1 + 2 * group + way).wait_recv()
                if way == (part + group) % 2 and not (group == 1 and FAR_BY_MATE):
                    g_copy(it, kind, part, 5 + group).start()
                split_b(it, kind, part, g_slot(group, 2 * way - 1))

        def from_far(kind, part, group):
            g_copy(it, kind, part, 5 + group).wait_recv()
            if group == 0 and FAR_BY_MATE:
                g_copy(it, kind, part, 6).start()
            split_b(it, kind, part, g_slot(group, 2))

        def square(part):
            rows = slice(part * TILE, (part + 1) * TILE)
            value = dot3(a_hi[rows, :], a_lo[rows, :], b_hi[...], b_lo[...])
            sq_part[it, part, 0] = value[:DEPTH]
            sq_part[it, part, 1] = value[DEPTH:]
            e_copy(it, part).start()

        def square_ready(part):
            e_copy(it, part).wait_recv()
            value = sq_part[it, part, layer] + sq_from[it, part]
            s_in[it, row, part] = tile_mask(filters, (it, 2 * (part // 2) + layer), value)
            for what in range(7 if part in STRAIGHT else 3):
                g_copy(it, "S", part, what).start()
            split_b(it, "S", part, row)

        def product(first, part):
            rows = slice(part * 256, (part + 1) * 256)
            depth = slice(0, 1024) if first else slice(1024, 2048)
            value = dot3(a_hi[rows, depth], a_lo[rows, depth], s_hi[depth, :], s_lo[depth, :])
            if first:
                pr_part[it, rows, :] = value
            else:
                pr_part[it, rows, :] += value
                pr_copy(it, part).start()

        def update(part):
            pr_copy(it, part).wait_recv()
            for half in range(2):
                for side in range(2):
                    at = (4 * part + 2 * half + side) * DEPTH
                    rows = slice(at, at + DEPTH)
                    place = (part, side, half)
                    if it < ITERS - 1:
                        value = tile_mask(filters, (it, 2 * part + side), pr_part[it, rows, :] + pr_from[it, rows, :])
                        own[place] = 1.5 * own[place] - 0.5 * value
                    else:
                        value = (pr_part[it, rows, mine] + pr_from[it, rows, mine]) * filters[
                            it, 2 * part + side, layer
                        ].astype(F32)
                        out[place] = 1.5 * own[(*place, slice(None), mine)] - 0.5 * value

        run = {
            "y": y_begin, "zb": z_begin, "yb": y_arrives, "z": z_arrives, "bg": column_begin, "gm": from_mate,
            "gn": from_near, "gf": from_far, "gd": straight, "sq": square, "sr": square_ready,
            "pr0": lambda part: product(True, part),
        }
        for step in STEPS:
            run[step[0]](*step[1:])
        product(False, 0)
        product(False, 1)
        return update

    def drain(it):
        for k in range(PARTS):
            for group in range(2):
                for way in range(2):
                    for depth in range(4):
                        if depth < 3 or way == far_way(group, k):
                            if group == 0 or k not in BY_PARTNER:
                                z_copy(it, group, k, way, depth).wait_send()
                            if group == 0 and k in BY_PARTNER:
                                p_copy(it, k, way, depth + 1).wait_send()
            for kind in "BS":
                for what in range(7):
                    g_copy(it, kind, k, what).wait_send()
            y_copy(it, k).wait_send()
            e_copy(it, k).wait_send()
        pr_copy(it, 0).wait_send()
        pr_copy(it, 1).wait_send()

    for tile in range(4):
        for half in range(2):
            place = (tile // 2, tile % 2, half)
            own[place] = tile_mask(pattern, (tile,), initial[place])
    pl.semaphore_wait(barrier, len(neighbours))
    for part in range(PARTS):
        own_part(0, part)
    for it in range(ITERS):
        update = iteration(it)
        for part in range(2):
            update(part)
            if it + 1 < ITERS:
                own_part(it + 1, 2 * part)
                own_part(it + 1, 2 * part + 1)
    for it in range(ITERS):
        drain(it)


def on_device(initial, pattern, filters):
    dma = pltpu.SemaphoreType.DMA
    vmem = pltpu.VMEM
    out = pl.pallas_call(
        kernel,
        out_shape=jax.ShapeDtypeStruct((2, 2, 2, DEPTH, TILE), F32),
        in_specs=[
            pl.BlockSpec(memory_space=pltpu.VMEM),
            pl.BlockSpec(memory_space=pltpu.SMEM),
            pl.BlockSpec(memory_space=pltpu.SMEM),
        ],
        out_specs=pl.BlockSpec(memory_space=pltpu.VMEM),
        scratch_shapes=[
            vmem((2, 2, 2, DEPTH, 256), F32),
            vmem((ITERS, 16, 2, 2, 2, DEPTH, TILE), F32),
            vmem((ITERS, 8, PARTS, DEPTH, 256), F32),
            vmem((ITERS, 8, PARTS, DEPTH, 256), F32),
            vmem((512, 2048), BF16),
            vmem((512, 2048), BF16),
            vmem((2048, 256), BF16),
            vmem((2048, 256), BF16),
            vmem((2048, 256), BF16),
            vmem((2048, 256), BF16),
            vmem((ITERS, PARTS, 2, DEPTH, 256), F32),
            vmem((ITERS, PARTS, DEPTH, 256), F32),
            vmem((ITERS, 512, 256), F32),
            vmem((ITERS, 512, 256), F32),
            dma((ITERS, 2, PARTS, 2, 4)),
            dma((ITERS, 2, PARTS, 2, 4)),
            dma((ITERS, PARTS)),
            dma((ITERS, PARTS)),
            dma((ITERS, max(1, len(BY_PARTNER)), 2, 4)),
            dma((ITERS, max(1, len(BY_PARTNER)), 2, 4)),
            dma((ITERS, 2, PARTS, 7)),
            dma((ITERS, 2, PARTS, 7)),
            dma((ITERS, PARTS + 2)),
            dma((ITERS, PARTS + 2)),
        ],
        compiler_params=pltpu.CompilerParams(
            collective_id=0, has_side_effects=True, vmem_limit_bytes=52 << 20
        ),
        name="sign_iterations",
    )(initial.reshape(2, 2, 2, DEPTH, 256), pattern, filters)
    return out.reshape(512, TILE)


def solution(mesh):
    return jax.shard_map(
        on_device,
        mesh=mesh,
        in_specs=(P("row", "col"), P("row", "col"), P(None, "row", "col")),
        out_specs=P("row", ("col", "layer")),
        check_vma=False,
    )
```

```python
import jax
import jax.numpy as jnp
from jax import lax
from jax.experimental import pallas as pl
from jax.experimental.pallas import tpu as pltpu
from jax.sharding import PartitionSpec as P

MESH = pl.DeviceIdType.MESH
TILE = 128
ITERS = 2
SIZES = (64, 64, 64, 32, 32)
PARTS = len(SIZES)
STARTS = tuple(sum(SIZES[:k]) for k in range(PARTS))
F32 = jnp.float32
BF16 = jnp.bfloat16
BY_PARTNER = (1,)
FAR_BY_MATE = "S"
STRAIGHT = (4,)
STEPS = [
    ("ox", 0), ("zb", 1), ("y", 0), ("ox", 1), ("zb", 3), ("bg", 4), ("y", 3), ("zb", 2), ("y", 4), ("zb", 0),
    ("bg", 2), ("bg", 3), ("bg", 0), ("yb", 0), ("gm", "B", 4), ("y", 1), ("y", 2), ("bg", 1), ("gn", "B", 4, 0),
    ("z", 0, 3, 1), ("z", 0, 1, 1), ("gn", "B", 2, 0), ("z", 0, 0, 1), ("gm", "B", 2), ("gm", "B", 3), ("yb", 3),
    ("yb", 4), ("z", 1, 0, 1), ("z", 0, 1, 2), ("gn", "B", 1, 0), ("gm", "B", 0), ("yb", 2), ("gn", "B", 0, 0),
    ("z", 1, 3, 1), ("gf", "B", 4, 0), ("z", 0, 0, 2), ("gn", "B", 3, 0), ("gm", "B", 1), ("z", 0, 1, 3),
    ("gn", "B", 0, 1), ("yb", 1), ("gn", "B", 3, 1), ("gn", "B", 4, 1), ("z", 1, 0, 2), ("z", 1, 2, 1),
    ("gn", "B", 1, 1), ("z", 1, 3, 2), ("z", 0, 3, 2), ("gn", "B", 2, 1), ("z", 0, 2, 1), ("z", 0, 1, 4),
    ("gf", "B", 4, 1), ("gf", "B", 2, 0), ("z", 0, 0, 3), ("z", 1, 1, 1), ("z", 1, 0, 3), ("gf", "B", 3, 1),
    ("gf", "B", 1, 0), ("z", 1, 1, 2), ("gf", "B", 0, 0), ("gf", "B", 1, 1), ("gf", "B", 3, 0), ("gf", "B", 2, 1),
    ("z", 1, 1, 3), ("z", 1, 2, 2), ("z", 1, 3, 3), ("z", 1, 1, 4), ("zb", 4), ("gf", "B", 0, 1), ("sq", 1),
    ("z", 0, 3, 3), ("z", 1, 4, 1), ("z", 0, 0, 4), ("z", 0, 2, 2), ("sr", 1), ("z", 1, 0, 4), ("sq", 0),
    ("z", 0, 4, 1), ("z", 1, 3, 4), ("z", 1, 2, 3), ("sr", 0), ("z", 1, 4, 2), ("z", 0, 2, 3), ("gm", "S", 1),
    ("z", 0, 3, 4), ("sq", 3), ("gn", "S", 1, 0), ("z", 0, 4, 2), ("gn", "S", 0, 0), ("gm", "S", 0), ("sr", 3),
    ("z", 0, 2, 4), ("z", 1, 2, 4), ("sq", 2), ("z", 1, 4, 3), ("z", 0, 4, 3), ("sr", 2), ("gf", "S", 0, 0),
    ("gf", "S", 1, 0), ("z", 0, 4, 4), ("gm", "S", 3), ("z", 1, 4, 4), ("sq", 4), ("gn", "S", 3, 0),
    ("gn", "S", 2, 0), ("sr", 4), ("gn", "S", 1, 1), ("gn", "S", 0, 1), ("gf", "S", 3, 0), ("gn", "S", 3, 1),
    ("gf", "S", 2, 0), ("gm", "S", 2), ("gd", "S", 4, 0), ("gf", "S", 1, 1), ("gf", "S", 0, 1), ("pr0", 0),
    ("pr0", 1), ("gf", "S", 3, 1), ("gd", "S", 4, 1), ("gn", "S", 2, 1), ("gf", "S", 2, 1),
]


def halves(value):
    high = value.astype(BF16)
    return high, (value - high.astype(F32)).astype(BF16)


def dot3(a_high, a_low, b_high, b_low):
    def dot(a, b):
        return jnp.dot(a, b, preferred_element_type=F32)

    return dot(a_high, b_high) + (dot(a_high, b_low) + dot(a_low, b_high))


def kernel(
    initial, pattern_in, filters_in, out,
    raw, pattern, filters, own, a_in, b_in, s_in, a_hi, a_lo, b_hi, b_lo, s_hi, s_lo, sq_part, sq_from, pr_part, pr_from,
    sent, a_recv, y_recv, p_recv, g_recv, e_recv, in_sem,
):
    row, col, layer = lax.axis_index("row"), lax.axis_index("col"), lax.axis_index("layer")
    x, y_lo = lax.rem(row, 4), row // 4
    z, y_hi = col // 2, lax.rem(col, 2)
    def at_x(step):
        return {"row": y_lo * 4 + lax.rem(x + step + 4, 4)}

    def at_z(step):
        return {"col": lax.rem(z + step + 8, 8) * 2 + y_hi}

    def mate_x(step):
        return {"row": (1 - y_lo) * 4 + lax.rem(x + step + 4, 4)}

    mate_lo = mate_x(0)
    mate_hi = {"col": z * 2 + (1 - y_hi)}
    sibling = {"layer": 1 - layer}

    barrier = pltpu.get_barrier_semaphore()
    neighbours = (at_x(1), at_x(-1), at_z(1), at_z(-1), mate_lo, mate_hi, sibling)
    if STRAIGHT:
        neighbours += (at_x(2), mate_x(1), mate_x(-1), mate_x(2))
    for device in neighbours:
        pl.semaphore_signal(barrier, inc=1, device_id=device, device_id_type=MESH)

    def half_of(k):
        return STARTS[k] // TILE

    def span(k):
        return pl.ds(STARTS[k] % TILE, SIZES[k])

    def tile_mask(ref, index, value):
        parts = []
        for ct in range(2):
            parts.append(value[:, ct * TILE : (ct + 1) * TILE] * ref[(*index, ct)].astype(F32))
        return jnp.concatenate(parts, axis=1)

    def remote(src, dst, send, recv, device):
        return pltpu.make_async_remote_copy(
            src_ref=src, dst_ref=dst, send_sem=send, recv_sem=recv, device_id=device, device_id_type=MESH
        )

    def z_slot(group, way, depth):
        at = lax.rem(z - depth + 8, 8) if way == 0 else lax.rem(z + depth, 8)
        return 2 * at + (y_hi if group == 0 else 1 - y_hi)

    def far_way(group, k):
        return k % 2 if k in BY_PARTNER else (k + group) % 2

    def a_piece(it, k, slot):
        return a_in.at[it, slot, pl.ds(2 * STARTS[k], 2 * SIZES[k])]

    def z_copy(it, group, k, way, depth):
        piece = a_piece(it, k, z_slot(group, way, depth))
        return remote(piece, piece, sent.at[0], a_recv.at[it, group, k, depth], at_z(1 - 2 * way))

    def a_wait(it, k, depth, recv):
        pieces = a_in.at[it, pl.ds(0, 1 if depth == 4 else 2), pl.ds(2 * STARTS[k], 2 * SIZES[k])]
        remote(pieces, pieces, sent.at[0], recv, mate_hi).wait_recv()

    def y_copy(it, k):
        piece = a_piece(it, k, col)
        return remote(piece, piece, sent.at[0], y_recv.at[it, k], mate_hi)

    def p_copy(it, k, way, depth):
        piece = a_piece(it, k, z_slot(0, way, depth))
        return remote(piece, piece, sent.at[0], p_recv.at[it, BY_PARTNER.index(k), depth - 1], mate_hi)

    def split_a(it, k, slot):
        columns = pl.ds(pl.multiple_of(lax.rem(slot, 2) * 1024 + slot // 2 * TILE, TILE), TILE)
        rows = slice(2 * STARTS[k], 2 * (STARTS[k] + SIZES[k]))
        high, low = halves(a_in[it, slot, rows])
        a_hi[rows, columns] = high
        a_lo[rows, columns] = low

    bufs = {"B": (b_in, b_hi, b_lo), "S": (s_in, s_hi, s_lo)}

    def split_b(it, kind, part, slot):
        buf, high_ref, low_ref = bufs[kind]
        high, low = halves(buf[it, slot, half_of(part), span(part)])
        rows = pl.ds(pl.multiple_of(half_of(part) * 1024 + slot * TILE + STARTS[part] % TILE, 16), SIZES[part])
        high_ref[rows, :] = high
        low_ref[rows, :] = low

    def g_slot(group, step):
        lane = y_lo if group == 0 else 1 - y_lo
        return lane * 4 + lax.rem(x + step + 4, 4)

    def g_copy(it, kind, part, what):
        way = (part + what - 5) % 2
        if kind == "S" and part in STRAIGHT:
            slot = row
            device = (mate_lo, at_x(1), at_x(-1), mate_x(1), mate_x(-1), at_x(2), mate_x(2))[what]
        elif what == 0:
            slot, device = g_slot(0, 0), mate_lo
        elif what < 5:
            slot, device = g_slot((what - 1) // 2, 0), at_x(1 if what % 2 else -1)
        elif what == 6 and kind in FAR_BY_MATE:
            slot, device = g_slot(0, 2), mate_lo
        else:
            slot, device = g_slot(what - 5, 2 * way - 1), at_x(1 - 2 * way)
        piece = bufs[kind][0].at[it, slot, half_of(part), span(part)]
        return remote(piece, piece, sent.at[1 + "BS".index(kind)], g_sem(it, kind, part, what), device)

    def g_sem(it, kind, part, what):
        straight_on = kind == "S" and part in STRAIGHT
        return g_recv.at[it, "BS".index(kind), part, int(what > 2) if straight_on else (0, 1, 1, 2, 2, 3, 4)[what]]

    def g_wait(it, kind, part, what, count):
        pieces = bufs[kind][0].at[it, pl.ds(0, count), half_of(part), span(part)]
        remote(pieces, pieces, sent.at[1 + "BS".index(kind)], g_sem(it, kind, part, what), mate_lo).wait_recv()

    def rows_of(part):
        return pl.ds(STARTS[part], SIZES[part])

    def e_copy(it, part):
        return remote(
            sq_part.at[it, 1 - layer, rows_of(part)], sq_from.at[it, rows_of(part)], sent.at[3], e_recv.at[it, part], sibling
        )

    def pr_copy(it, part):
        rows = pl.ds(part * 256, 256)
        columns = slice(None)
        if it == ITERS - 1:
            columns = pl.ds(pl.multiple_of((1 - layer) * TILE, TILE), TILE)
        return remote(
            pr_part.at[it, rows, columns], pr_from.at[it, rows, columns],
            sent.at[4 + it], e_recv.at[it, PARTS + part], sibling,
        )

    mine = pl.ds(pl.multiple_of(layer * TILE, TILE), TILE)

    def own_part(it, part):
        for side in range(2):
            rows = pl.ds(2 * STARTS[part] + side * SIZES[part], SIZES[part])
            a_in[it, col, rows] = own[half_of(part), side, span(part), mine]
        split_a(it, part, col)
        b_in[it, row, half_of(part), span(part)] = own[half_of(part), layer, span(part)]
        split_b(it, "B", part, row)

    def iteration(it, update_before):
        def y_begin(k):
            y_copy(it, k).start()

        def z_begin(k):
            z_copy(it, 0, k, 0, 0).start()
            z_copy(it, 0, k, 1, 0).start()

        def y_arrives(k):
            y_copy(it, k).wait_recv()
            if k not in BY_PARTNER:
                z_copy(it, 1, k, 0, 0).start()
                z_copy(it, 1, k, 1, 0).start()
            split_a(it, k, z_slot(1, 0, 0))

        def z_arrives(group, k, depth):
            ways = [way for way in range(2) if depth < 4 or way == far_way(group, k)]
            if group == 1 and k in BY_PARTNER:
                a_wait(it, k, depth, p_recv.at[it, BY_PARTNER.index(k), depth - 1])
            else:
                a_wait(it, k, depth, a_recv.at[it, group, k, depth - 1])
                for way in ways:
                    if depth < 3 or (depth == 3 and way == far_way(group, k)):
                        z_copy(it, group, k, way, depth).start()
                    if k in BY_PARTNER:
                        p_copy(it, k, way, depth).start()
            for way in ways:
                split_a(it, k, z_slot(group, way, depth))

        def column_begin(part):
            for what in range(3):
                g_copy(it, "B", part, what).start()

        def straight(kind, part, far):
            whats = (3, 4, 5, 6) if far else (0, 1, 2)
            g_wait(it, kind, part, whats[0], len(whats))
            slots = (g_slot(1, 0), g_slot(0, -1), g_slot(0, 1), g_slot(1, -1), g_slot(1, 1), g_slot(0, 2), g_slot(1, 2))
            for what in whats:
                split_b(it, kind, part, slots[what])

        def from_mate(kind, part):
            g_wait(it, kind, part, 0, 1)
            g_copy(it, kind, part, 3).start()
            g_copy(it, kind, part, 4).start()
            split_b(it, kind, part, g_slot(1, 0))

        def from_near(kind, part, group):
            g_wait(it, kind, part, 1 + 2 * group, 2)
            for way in range(2):
                if way == (part + group) % 2 and not (group == 1 and kind in FAR_BY_MATE):
                    g_copy(it, kind, part, 5 + group).start()
                split_b(it, kind, part, g_slot(group, 2 * way - 1))

        def from_far(kind, part, group):
            g_wait(it, kind, part, 5 + group, 1)
            if group == 0 and kind in FAR_BY_MATE:
                g_copy(it, kind, part, 6).start()
            split_b(it, kind, part, g_slot(group, 2))

        def square(part):
            rows = slice(2 * STARTS[part], 2 * (STARTS[part] + SIZES[part]))
            value = dot3(a_hi[rows, :], a_lo[rows, :], b_hi[...], b_lo[...])
            sq_part[it, 0, rows_of(part)] = value[: SIZES[part]]
            sq_part[it, 1, rows_of(part)] = value[SIZES[part] :]
            e_copy(it, part).start()

        def square_ready(part):
            e_copy(it, part).wait_recv()
            value = sq_part[it, layer, rows_of(part)] + sq_from[it, rows_of(part)]
            s_in[it, row, half_of(part), span(part)] = tile_mask(filters, (it, 2 * half_of(part) + layer), value)
            for what in range(7 if part in STRAIGHT else 3):
                g_copy(it, "S", part, what).start()
            split_b(it, "S", part, row)

        def product(first, part):
            rows = slice(part * 256, (part + 1) * 256)
            depth = slice(0, 1024) if first else slice(1024, 2048)
            value = dot3(a_hi[rows, depth], a_lo[rows, depth], s_hi[depth, :], s_lo[depth, :])
            if first:
                pr_part[it, rows, :] = value
            else:
                pr_part[it, rows, :] += value
                pr_copy(it, part).start()

        def update(part):
            pr_copy(it, part).wait_recv()
            for k in range(PARTS):
                for side in range(2):
                    if half_of(k) != part:
                        continue
                    at = 2 * STARTS[k] + side * SIZES[k]
                    rows = slice(at, at + SIZES[k])
                    place = (part, side, span(k))
                    if it < ITERS - 1:
                        value = tile_mask(filters, (it, 2 * part + side), pr_part[it, rows, :] + pr_from[it, rows, :])
                        own[place] = 1.5 * own[place] - 0.5 * value
                    else:
                        value = (pr_part[it, rows, mine] + pr_from[it, rows, mine]) * filters[
                            it, 2 * part + side, layer
                        ].astype(F32)
                        out[place] = 1.5 * own[(*place, mine)] - 0.5 * value

        def own_half(part):
            if update_before is not None:
                update_before(part)
            else:
                for side in range(2):
                    own[part, side] = tile_mask(pattern, (2 * part + side,), raw[part, side])
            for k in range(PARTS):
                if half_of(k) == part:
                    own_part(it, k)

        run = {
            "ox": own_half,
            "y": y_begin, "zb": z_begin, "yb": y_arrives, "z": z_arrives, "bg": column_begin, "gm": from_mate,
            "gn": from_near, "gf": from_far, "gd": straight, "sq": square, "sr": square_ready,
            "pr0": lambda part: product(True, part),
        }
        for step in STEPS:
            run[step[0]](*step[1:])
        product(False, 0)
        product(False, 1)
        return update

    fetch = [
        pltpu.make_async_copy(src, dst, in_sem.at[index])
        for index, (src, dst) in enumerate(((initial, raw), (pattern_in, pattern), (filters_in, filters)))
    ]
    for copy in fetch:
        copy.start()
    for copy in fetch:
        copy.wait()
    pl.semaphore_wait(barrier, len(neighbours))
    before = None
    for it in range(ITERS):
        before = iteration(it, before)
    before(0)
    before(1)
    pieces = (a_in.at[:, pl.ds(0, 15)], b_in.at[:, pl.ds(0, 7)], s_in.at[:, pl.ds(0, 7)], sq_from, pr_from.at[0], pr_from.at[1, :, mine])
    for index, piece in enumerate(pieces):
        remote(piece, piece, sent.at[index], in_sem.at[0], sibling).wait_send()


def on_device(initial, pattern, filters):
    dma = pltpu.SemaphoreType.DMA
    vmem = pltpu.VMEM
    out = pl.pallas_call(
        kernel,
        out_shape=jax.ShapeDtypeStruct((2, 2, TILE, TILE), F32),
        in_specs=[
            pl.BlockSpec(memory_space=pltpu.HBM),
            pl.BlockSpec(memory_space=pl.ANY),
            pl.BlockSpec(memory_space=pl.ANY),
        ],
        out_specs=pl.BlockSpec(memory_space=pltpu.VMEM),
        scratch_shapes=[
            vmem((2, 2, TILE, 256), F32),
            pltpu.SMEM((4, 2), jnp.int32),
            pltpu.SMEM((ITERS, 4, 2), jnp.int32),
            vmem((2, 2, TILE, 256), F32),
            vmem((ITERS, 16, 512, TILE), F32),
            vmem((ITERS, 8, 2, TILE, 256), F32),
            vmem((ITERS, 8, 2, TILE, 256), F32),
            vmem((512, 2048), BF16),
            vmem((512, 2048), BF16),
            vmem((2048, 256), BF16),
            vmem((2048, 256), BF16),
            vmem((2048, 256), BF16),
            vmem((2048, 256), BF16),
            vmem((ITERS, 2, 256, 256), F32),
            vmem((ITERS, 256, 256), F32),
            vmem((ITERS, 512, 256), F32),
            vmem((ITERS, 512, 256), F32),
            dma((4 + ITERS,)),
            dma((ITERS, 2, PARTS, 4)),
            dma((ITERS, PARTS)),
            dma((ITERS, max(1, len(BY_PARTNER)), 4)),
            dma((ITERS, 2, PARTS, 5)),
            dma((ITERS, PARTS + 2)),
            dma((3,)),
        ],
        compiler_params=pltpu.CompilerParams(
            collective_id=0, has_side_effects=True, vmem_limit_bytes=40 << 20
        ),
        name="sign_iterations",
    )(initial.reshape(2, 2, TILE, 256), pattern, filters)
    return out.reshape(512, TILE)


def solution(mesh):
    return jax.shard_map(
        on_device,
        mesh=mesh,
        in_specs=(P("row", "col"), P("row", "col"), P(None, "row", "col")),
        out_specs=P("row", ("col", "layer")),
        check_vma=False,
    )
```

```python
import jax
import jax.numpy as jnp
from jax import lax
from jax.experimental import pallas as pl
from jax.experimental.pallas import tpu as pltpu
from jax.sharding import PartitionSpec as P

MESH = pl.DeviceIdType.MESH
TILE = 128
ITERS = 2
SIZES = (64, 64, 64, 32, 32)
PARTS = len(SIZES)
STARTS = tuple(sum(SIZES[:k]) for k in range(PARTS))
F32 = jnp.float32
BF16 = jnp.bfloat16
BY_PARTNER = (1, 3)
FAR_BY_MATE = "S"
STRAIGHT = {"B": (), "S": (4,)}
STEPS = [
    ("ox", 0), ("zb", 0), ("y", 0), ("zb", 1), ("ox", 1), ("bg", 1), ("bg", 0), ("bg", 3), ("zb", 3), ("zb", 2),
    ("y", 2), ("yb", 0), ("z", 0, 0, 1), ("gm", "B", 1), ("bg", 2), ("z", 0, 3, 1), ("z", 0, 1, 1), ("gm", "B", 3),
    ("gn", "B", 0, 0), ("gm", "B", 0), ("yb", 2), ("gn", "B", 1, 0), ("z", 1, 0, 1), ("bg", 4), ("gn", "B", 3, 0),
    ("z", 0, 3, 2), ("z", 0, 0, 2), ("y", 1), ("gm", "B", 2), ("z", 0, 1, 2), ("z", 1, 2, 1), ("gn", "B", 2, 0),
    ("gm", "B", 4), ("gn", "B", 0, 1), ("gn", "B", 4, 0), ("y", 3), ("y", 4), ("z", 1, 0, 2), ("gn", "B", 1, 1),
    ("gf", "B", 3, 0), ("gn", "B", 2, 1), ("z", 0, 2, 1), ("z", 0, 1, 3), ("yb", 1), ("gn", "B", 4, 1),
    ("gn", "B", 3, 1), ("gf", "B", 0, 1), ("z", 0, 0, 3), ("z", 1, 1, 1), ("z", 0, 3, 3), ("z", 1, 0, 3),
    ("zb", 4), ("gf", "B", 0, 0), ("gf", "B", 2, 0), ("gf", "B", 1, 1), ("yb", 4), ("yb", 3), ("gf", "B", 1, 0),
    ("gf", "B", 2, 1), ("z", 1, 2, 2), ("gf", "B", 4, 0), ("gf", "B", 4, 1), ("gf", "B", 3, 1), ("z", 1, 3, 1),
    ("z", 0, 1, 4), ("z", 0, 0, 4), ("z", 0, 2, 2), ("z", 1, 1, 2), ("z", 0, 3, 4), ("z", 1, 1, 3), ("z", 1, 0, 4),
    ("sq", 0), ("z", 1, 3, 2), ("z", 1, 4, 1), ("z", 0, 4, 1), ("z", 1, 1, 4), ("sr", 0), ("sq", 1),
    ("z", 1, 2, 3), ("z", 0, 2, 3), ("sr", 1), ("z", 1, 3, 3), ("z", 1, 3, 4), ("z", 1, 4, 2), ("sq", 3),
    ("gm", "S", 0), ("z", 0, 4, 2), ("gn", "S", 0, 0), ("sr", 3), ("z", 1, 2, 4), ("z", 0, 2, 4), ("sq", 2),
    ("gn", "S", 1, 0), ("z", 1, 4, 3), ("sr", 2), ("z", 0, 4, 3), ("gf", "S", 0, 0), ("gm", "S", 3),
    ("gm", "S", 1), ("gn", "S", 3, 0), ("z", 1, 4, 4), ("z", 0, 4, 4), ("sq", 4), ("gf", "S", 1, 0),
    ("gn", "S", 2, 0), ("sr", 4), ("gn", "S", 1, 1), ("gf", "S", 1, 1), ("gn", "S", 0, 1), ("gn", "S", 3, 1),
    ("gf", "S", 3, 0), ("gf", "S", 0, 1), ("gm", "S", 2), ("gf", "S", 2, 0), ("gd", "S", 4, 0), ("pr0", 1),
    ("pr0", 0), ("gf", "S", 3, 1), ("gd", "S", 4, 1), ("gn", "S", 2, 1), ("gf", "S", 2, 1),
]


def halves(value):
    high = value.astype(BF16)
    return high, (value - high.astype(F32)).astype(BF16)


def dot3(a_high, a_low, b_high, b_low):
    def dot(a, b):
        return jnp.dot(a, b, preferred_element_type=F32)

    return dot(a_high, b_high) + (dot(a_high, b_low) + dot(a_low, b_high))


def kernel(
    initial, pattern_in, filters_in, out,
    raw, pattern, filters, own, a_in, b_in, s_in, a_hi, a_lo, b_hi, b_lo, s_hi, s_lo, sq_part, sq_from, pr_part, pr_from,
    sent, a_recv, y_recv, p_recv, g_recv, e_recv, in_sem,
):
    row, col, layer = lax.axis_index("row"), lax.axis_index("col"), lax.axis_index("layer")
    x, y_lo = lax.rem(row, 4), row // 4
    z, y_hi = col // 2, lax.rem(col, 2)
    def at_x(step):
        return {"row": y_lo * 4 + lax.rem(x + step + 4, 4)}

    def at_z(step):
        return {"col": lax.rem(z + step + 8, 8) * 2 + y_hi}

    def mate_x(step):
        return {"row": (1 - y_lo) * 4 + lax.rem(x + step + 4, 4)}

    mate_lo = mate_x(0)
    mate_hi = {"col": z * 2 + (1 - y_hi)}
    sibling = {"layer": 1 - layer}

    barrier = pltpu.get_barrier_semaphore()
    neighbours = (at_x(1), at_x(-1), at_z(1), at_z(-1), mate_lo, mate_hi, sibling)
    if any(STRAIGHT.values()):
        neighbours += (at_x(2), mate_x(1), mate_x(-1), mate_x(2))
    for device in neighbours:
        pl.semaphore_signal(barrier, inc=1, device_id=device, device_id_type=MESH)

    def half_of(k):
        return STARTS[k] // TILE

    def span(k):
        return pl.ds(STARTS[k] % TILE, SIZES[k])

    def tile_mask(ref, index, value):
        parts = []
        for ct in range(2):
            parts.append(value[:, ct * TILE : (ct + 1) * TILE] * ref[(*index, ct)].astype(F32))
        return jnp.concatenate(parts, axis=1)

    def remote(src, dst, send, recv, device):
        return pltpu.make_async_remote_copy(
            src_ref=src, dst_ref=dst, send_sem=send, recv_sem=recv, device_id=device, device_id_type=MESH
        )

    def z_slot(group, way, depth):
        at = lax.rem(z - depth + 8, 8) if way == 0 else lax.rem(z + depth, 8)
        return 2 * at + (y_hi if group == 0 else 1 - y_hi)

    def far_way(group, k):
        return k % 2 if k in BY_PARTNER else (k + group) % 2

    def a_piece(it, k, slot):
        return a_in.at[it, slot, pl.ds(2 * STARTS[k], 2 * SIZES[k])]

    def z_copy(it, group, k, way, depth):
        piece = a_piece(it, k, z_slot(group, way, depth))
        return remote(piece, piece, sent.at[0], a_recv.at[it, group, k, depth], at_z(1 - 2 * way))

    def a_wait(it, k, depth, recv):
        pieces = a_in.at[it, pl.ds(0, 1 if depth == 4 else 2), pl.ds(2 * STARTS[k], 2 * SIZES[k])]
        remote(pieces, pieces, sent.at[0], recv, mate_hi).wait_recv()

    def y_copy(it, k):
        piece = a_piece(it, k, col)
        return remote(piece, piece, sent.at[0], y_recv.at[it, k], mate_hi)

    def p_copy(it, k, way, depth):
        piece = a_piece(it, k, z_slot(0, way, depth))
        return remote(piece, piece, sent.at[0], p_recv.at[it, BY_PARTNER.index(k), depth - 1], mate_hi)

    def split_a(it, k, slot):
        columns = pl.ds(pl.multiple_of(lax.rem(slot, 2) * 1024 + slot // 2 * TILE, TILE), TILE)
        rows = slice(2 * STARTS[k], 2 * (STARTS[k] + SIZES[k]))
        high, low = halves(a_in[it, slot, rows])
        a_hi[rows, columns] = high
        a_lo[rows, columns] = low

    bufs = {"B": (b_in, b_hi, b_lo), "S": (s_in, s_hi, s_lo)}

    def split_b(it, kind, part, slot):
        buf, high_ref, low_ref = bufs[kind]
        high, low = halves(buf[it, slot, half_of(part), span(part)])
        rows = pl.ds(pl.multiple_of(half_of(part) * 1024 + slot * TILE + STARTS[part] % TILE, 16), SIZES[part])
        high_ref[rows, :] = high
        low_ref[rows, :] = low

    def g_slot(group, step):
        lane = y_lo if group == 0 else 1 - y_lo
        return lane * 4 + lax.rem(x + step + 4, 4)

    def g_copy(it, kind, part, what):
        way = (part + what - 5) % 2
        if part in STRAIGHT[kind]:
            slot = row
            device = (mate_lo, at_x(1), at_x(-1), mate_x(1), mate_x(-1), at_x(2), mate_x(2))[what]
        elif what == 0:
            slot, device = g_slot(0, 0), mate_lo
        elif what < 5:
            slot, device = g_slot((what - 1) // 2, 0), at_x(1 if what % 2 else -1)
        elif what == 6 and kind in FAR_BY_MATE:
            slot, device = g_slot(0, 2), mate_lo
        else:
            slot, device = g_slot(what - 5, 2 * way - 1), at_x(1 - 2 * way)
        piece = bufs[kind][0].at[it, slot, half_of(part), span(part)]
        return remote(piece, piece, sent.at[1 + "BS".index(kind)], g_sem(it, kind, part, what), device)

    def g_sem(it, kind, part, what):
        straight_on = part in STRAIGHT[kind]
        return g_recv.at[it, "BS".index(kind), part, int(what > 2) if straight_on else (0, 1, 1, 2, 2, 3, 4)[what]]

    def g_wait(it, kind, part, what, count):
        pieces = bufs[kind][0].at[it, pl.ds(0, count), half_of(part), span(part)]
        remote(pieces, pieces, sent.at[1 + "BS".index(kind)], g_sem(it, kind, part, what), mate_lo).wait_recv()

    def rows_of(part):
        return pl.ds(STARTS[part], SIZES[part])

    def e_copy(it, part):
        return remote(
            sq_part.at[it, 1 - layer, rows_of(part)], sq_from.at[it, rows_of(part)], sent.at[3], e_recv.at[it, part], sibling
        )

    def pr_copy(it, part):
        rows = pl.ds(part * 256, 256)
        columns = slice(None)
        if it == ITERS - 1:
            columns = pl.ds(pl.multiple_of((1 - layer) * TILE, TILE), TILE)
        return remote(
            pr_part.at[it, rows, columns], pr_from.at[it, rows, columns],
            sent.at[4 + it], e_recv.at[it, PARTS + part], sibling,
        )

    mine = pl.ds(pl.multiple_of(layer * TILE, TILE), TILE)

    def own_part(it, part):
        for side in range(2):
            rows = pl.ds(2 * STARTS[part] + side * SIZES[part], SIZES[part])
            a_in[it, col, rows] = own[half_of(part), side, span(part), mine]
        b_in[it, row, half_of(part), span(part)] = own[half_of(part), layer, span(part)]

    def own_parts(it, half):
        for k in range(PARTS):
            if half_of(k) == half:
                own_part(it, k)

    def iteration(it, update_before):
        def y_begin(k):
            y_copy(it, k).start()

        def z_begin(k):
            z_copy(it, 0, k, 0, 0).start()
            z_copy(it, 0, k, 1, 0).start()
            split_a(it, k, col)

        def y_arrives(k):
            y_copy(it, k).wait_recv()
            if k not in BY_PARTNER:
                z_copy(it, 1, k, 0, 0).start()
                z_copy(it, 1, k, 1, 0).start()
            split_a(it, k, z_slot(1, 0, 0))

        def z_arrives(group, k, depth):
            ways = [way for way in range(2) if depth < 4 or way == far_way(group, k)]
            if group == 1 and k in BY_PARTNER:
                a_wait(it, k, depth, p_recv.at[it, BY_PARTNER.index(k), depth - 1])
            else:
                a_wait(it, k, depth, a_recv.at[it, group, k, depth - 1])
                for way in ways:
                    if depth < 3 or (depth == 3 and way == far_way(group, k)):
                        z_copy(it, group, k, way, depth).start()
                    if k in BY_PARTNER:
                        p_copy(it, k, way, depth).start()
            for way in ways:
                split_a(it, k, z_slot(group, way, depth))

        def column_begin(part):
            for what in range(7 if part in STRAIGHT["B"] else 3):
                g_copy(it, "B", part, what).start()
            split_b(it, "B", part, row)

        def straight(kind, part, far):
            whats = (3, 4, 5, 6) if far else (0, 1, 2)
            g_wait(it, kind, part, whats[0], len(whats))
            slots = (g_slot(1, 0), g_slot(0, -1), g_slot(0, 1), g_slot(1, -1), g_slot(1, 1), g_slot(0, 2), g_slot(1, 2))
            for what in whats:
                split_b(it, kind, part, slots[what])

        def from_mate(kind, part):
            g_wait(it, kind, part, 0, 1)
            g_copy(it, kind, part, 3).start()
            g_copy(it, kind, part, 4).start()
            split_b(it, kind, part, g_slot(1, 0))

        def from_near(kind, part, group):
            g_wait(it, kind, part, 1 + 2 * group, 2)
            for way in range(2):
                if way == (part + group) % 2 and not (group == 1 and kind in FAR_BY_MATE):
                    g_copy(it, kind, part, 5 + group).start()
                split_b(it, kind, part, g_slot(group, 2 * way - 1))

        def from_far(kind, part, group):
            g_wait(it, kind, part, 5 + group, 1)
            if group == 0 and kind in FAR_BY_MATE:
                g_copy(it, kind, part, 6).start()
            split_b(it, kind, part, g_slot(group, 2))

        def square(part):
            rows = slice(2 * STARTS[part], 2 * (STARTS[part] + SIZES[part]))
            value = dot3(a_hi[rows, :], a_lo[rows, :], b_hi[...], b_lo[...])
            sq_part[it, 0, rows_of(part)] = value[: SIZES[part]]
            sq_part[it, 1, rows_of(part)] = value[SIZES[part] :]
            e_copy(it, part).start()

        def square_ready(part):
            e_copy(it, part).wait_recv()
            value = sq_part[it, layer, rows_of(part)] + sq_from[it, rows_of(part)]
            s_in[it, row, half_of(part), span(part)] = tile_mask(filters, (it, 2 * half_of(part) + layer), value)
            for what in range(7 if part in STRAIGHT["S"] else 3):
                g_copy(it, "S", part, what).start()
            split_b(it, "S", part, row)

        def product(first, part):
            rows = slice(part * 256, (part + 1) * 256)
            depth = slice(0, 1024) if first else slice(1024, 2048)
            value = dot3(a_hi[rows, depth], a_lo[rows, depth], s_hi[depth, :], s_lo[depth, :])
            if first:
                pr_part[it, rows, :] = value
            else:
                pr_part[it, rows, :] += value
                pr_copy(it, part).start()

        def update(part):
            pr_copy(it, part).wait_recv()
            for k in range(PARTS):
                for side in range(2):
                    if half_of(k) != part:
                        continue
                    at = 2 * STARTS[k] + side * SIZES[k]
                    rows = slice(at, at + SIZES[k])
                    place = (part, side, span(k))
                    if it < ITERS - 1:
                        value = tile_mask(filters, (it, 2 * part + side), pr_part[it, rows, :] + pr_from[it, rows, :])
                        own[place] = 1.5 * own[place] - 0.5 * value
                    else:
                        value = (pr_part[it, rows, mine] + pr_from[it, rows, mine]) * filters[
                            it, 2 * part + side, layer
                        ].astype(F32)
                        out[place] = 1.5 * own[(*place, mine)] - 0.5 * value

        def own_half(part):
            if update_before is not None:
                update_before(part)
                own_parts(it, part)

        run = {
            "ox": own_half,
            "y": y_begin, "zb": z_begin, "yb": y_arrives, "z": z_arrives, "bg": column_begin, "gm": from_mate,
            "gn": from_near, "gf": from_far, "gd": straight, "sq": square, "sr": square_ready,
            "pr0": lambda part: product(True, part),
        }
        for step in STEPS:
            run[step[0]](*step[1:])
        product(False, 0)
        product(False, 1)
        return update

    fetch = [
        pltpu.make_async_copy(src, dst, in_sem.at[index])
        for index, (src, dst) in enumerate(((initial, raw), (pattern_in, pattern), (filters_in, filters)))
    ]
    for copy in fetch:
        copy.start()
    for copy in fetch:
        copy.wait()
    for half in range(2):
        for side in range(2):
            own[half, side] = tile_mask(pattern, (2 * half + side,), raw[half, side])
        own_parts(0, half)
    pl.semaphore_wait(barrier, len(neighbours))
    before = None
    for it in range(ITERS):
        before = iteration(it, before)
    before(0)
    before(1)
    pieces = (a_in.at[:, pl.ds(0, 15)], b_in.at[:, pl.ds(0, 7)], s_in.at[:, pl.ds(0, 7)], sq_from, pr_from.at[0], pr_from.at[1, :, mine])
    for index, piece in enumerate(pieces):
        remote(piece, piece, sent.at[index], in_sem.at[0], sibling).wait_send()


def on_device(initial, pattern, filters):
    dma = pltpu.SemaphoreType.DMA
    vmem = pltpu.VMEM
    out = pl.pallas_call(
        kernel,
        out_shape=jax.ShapeDtypeStruct((2, 2, TILE, TILE), F32),
        in_specs=[
            pl.BlockSpec(memory_space=pltpu.HBM),
            pl.BlockSpec(memory_space=pl.ANY),
            pl.BlockSpec(memory_space=pl.ANY),
        ],
        out_specs=pl.BlockSpec(memory_space=pltpu.VMEM),
        scratch_shapes=[
            vmem((2, 2, TILE, 256), F32),
            pltpu.SMEM((4, 2), jnp.int32),
            pltpu.SMEM((ITERS, 4, 2), jnp.int32),
            vmem((2, 2, TILE, 256), F32),
            vmem((ITERS, 16, 512, TILE), F32),
            vmem((ITERS, 8, 2, TILE, 256), F32),
            vmem((ITERS, 8, 2, TILE, 256), F32),
            vmem((512, 2048), BF16),
            vmem((512, 2048), BF16),
            vmem((2048, 256), BF16),
            vmem((2048, 256), BF16),
            vmem((2048, 256), BF16),
            vmem((2048, 256), BF16),
            vmem((ITERS, 2, 256, 256), F32),
            vmem((ITERS, 256, 256), F32),
            vmem((ITERS, 512, 256), F32),
            vmem((ITERS, 512, 256), F32),
            dma((4 + ITERS,)),
            dma((ITERS, 2, PARTS, 4)),
            dma((ITERS, PARTS)),
            dma((ITERS, max(1, len(BY_PARTNER)), 4)),
            dma((ITERS, 2, PARTS, 5)),
            dma((ITERS, PARTS + 2)),
            dma((3,)),
        ],
        compiler_params=pltpu.CompilerParams(
            collective_id=0, has_side_effects=True, vmem_limit_bytes=40 << 20
        ),
        name="sign_iterations",
    )(initial.reshape(2, 2, TILE, 256), pattern, filters)
    return out.reshape(512, TILE)


def solution(mesh):
    return jax.shard_map(
        on_device,
        mesh=mesh,
        in_specs=(P("row", "col"), P("row", "col"), P(None, "row", "col")),
        out_specs=P("row", ("col", "layer")),
        check_vma=False,
    )
```

```python
import jax
import jax.numpy as jnp
from jax import lax
from jax.experimental import pallas as pl
from jax.experimental.pallas import tpu as pltpu
from jax.sharding import PartitionSpec as P

MESH = pl.DeviceIdType.MESH
TILE = 128
ITERS = 2
SIZES = (64, 64, 64, 32, 32)
PARTS = len(SIZES)
STARTS = tuple(sum(SIZES[:k]) for k in range(PARTS))
F32 = jnp.float32
BF16 = jnp.bfloat16
BY_PARTNER = (1, 3)
FAR_BY_MATE = "S"
STRAIGHT = {"B": (), "S": (4,)}
STEPS = [
    ("ox", 0), ("zb", 0), ("y", 0), ("zb", 1), ("ox", 1), ("bg", 1), ("bg", 0), ("bg", 3), ("zb", 3), ("zb", 2),
    ("y", 2), ("yb", 0), ("z", 0, 0, 1), ("gm", "B", 1), ("bg", 2), ("z", 0, 3, 1), ("z", 0, 1, 1), ("gm", "B", 3),
    ("gn", "B", 0, 0), ("gm", "B", 0), ("yb", 2), ("gn", "B", 1, 0), ("z", 1, 0, 1), ("bg", 4), ("gn", "B", 3, 0),
    ("z", 0, 3, 2), ("z", 0, 0, 2), ("y", 1), ("gm", "B", 2), ("z", 0, 1, 2), ("z", 1, 2, 1), ("gn", "B", 2, 0),
    ("gm", "B", 4), ("gn", "B", 0, 1), ("gn", "B", 4, 0), ("y", 3), ("y", 4), ("z", 1, 0, 2), ("gn", "B", 1, 1),
    ("gf", "B", 3, 0), ("gn", "B", 2, 1), ("z", 0, 2, 1), ("z", 0, 1, 3), ("yb", 1), ("gn", "B", 4, 1),
    ("gn", "B", 3, 1), ("gf", "B", 0, 1), ("z", 0, 0, 3), ("z", 1, 1, 1), ("z", 0, 3, 3), ("z", 1, 0, 3),
    ("zb", 4), ("gf", "B", 0, 0), ("gf", "B", 2, 0), ("gf", "B", 1, 1), ("yb", 4), ("yb", 3), ("gf", "B", 1, 0),
    ("gf", "B", 2, 1), ("z", 1, 2, 2), ("gf", "B", 4, 0), ("gf", "B", 4, 1), ("gf", "B", 3, 1), ("z", 1, 3, 1),
    ("z", 0, 1, 4), ("z", 0, 0, 4), ("z", 0, 2, 2), ("z", 1, 1, 2), ("z", 0, 3, 4), ("z", 1, 1, 3), ("z", 1, 0, 4),
    ("sq", 0), ("z", 1, 3, 2), ("z", 1, 4, 1), ("z", 0, 4, 1), ("z", 1, 1, 4), ("sr", 0), ("sq", 1),
    ("z", 1, 2, 3), ("z", 0, 2, 3), ("sr", 1), ("z", 1, 3, 3), ("z", 1, 3, 4), ("z", 1, 4, 2), ("sq", 3),
    ("gm", "S", 0), ("z", 0, 4, 2), ("gn", "S", 0, 0), ("sr", 3), ("z", 1, 2, 4), ("z", 0, 2, 4), ("sq", 2),
    ("gn", "S", 1, 0), ("z", 1, 4, 3), ("sr", 2), ("z", 0, 4, 3), ("gf", "S", 0, 0), ("gm", "S", 3),
    ("gm", "S", 1), ("gn", "S", 3, 0), ("z", 1, 4, 4), ("z", 0, 4, 4), ("sq", 4), ("gf", "S", 1, 0),
    ("gn", "S", 2, 0), ("sr", 4), ("gn", "S", 1, 1), ("gf", "S", 1, 1), ("gn", "S", 0, 1), ("gn", "S", 3, 1),
    ("gf", "S", 3, 0), ("gf", "S", 0, 1), ("gm", "S", 2), ("gf", "S", 2, 0), ("gd", "S", 4, 0), ("pr0", 1),
    ("pr0", 0), ("gf", "S", 3, 1), ("gd", "S", 4, 1), ("gn", "S", 2, 1), ("gf", "S", 2, 1),
]


def halves(value):
    high = value.astype(BF16)
    return high, (value - high.astype(F32)).astype(BF16)


def dot3(a_high, a_low, b_high, b_low):
    def dot(a, b):
        return jnp.dot(a, b, preferred_element_type=F32)

    return dot(a_high, b_high) + (dot(a_high, b_low) + dot(a_low, b_high))


def kernel(
    initial, pattern_in, filters_in, out,
    raw, pattern, filters, own, a_in, b_in, s_in, a_hi, a_lo, b_hi, b_lo, s_hi, s_lo, sq_part, sq_from, pr_part, pr_from,
    sent, a_recv, y_recv, p_recv, g_recv, e_recv, in_sem,
):
    row, col, layer = lax.axis_index("row"), lax.axis_index("col"), lax.axis_index("layer")
    x, y_lo = lax.rem(row, 4), row // 4
    z, y_hi = col // 2, lax.rem(col, 2)
    def at_x(step):
        return {"row": y_lo * 4 + lax.rem(x + step + 4, 4)}

    def at_z(step):
        return {"col": lax.rem(z + step + 8, 8) * 2 + y_hi}

    def mate_x(step):
        return {"row": (1 - y_lo) * 4 + lax.rem(x + step + 4, 4)}

    mate_lo = mate_x(0)
    mate_hi = {"col": z * 2 + (1 - y_hi)}
    sibling = {"layer": 1 - layer}

    barrier = pltpu.get_barrier_semaphore()
    neighbours = (at_x(1), at_x(-1), at_z(1), at_z(-1), mate_lo, mate_hi, sibling)
    if any(STRAIGHT.values()):
        neighbours += (at_x(2), mate_x(1), mate_x(-1), mate_x(2))
    for device in neighbours:
        pl.semaphore_signal(barrier, inc=1, device_id=device, device_id_type=MESH)

    def half_of(k):
        return STARTS[k] // TILE

    def span(k):
        return pl.ds(STARTS[k] % TILE, SIZES[k])

    def tile_mask(ref, index, value):
        parts = []
        for ct in range(2):
            parts.append(value[:, ct * TILE : (ct + 1) * TILE] * ref[(*index, ct)].astype(F32))
        return jnp.concatenate(parts, axis=1)

    def remote(src, dst, send, recv, device):
        return pltpu.make_async_remote_copy(
            src_ref=src, dst_ref=dst, send_sem=send, recv_sem=recv, device_id=device, device_id_type=MESH
        )

    def z_slot(group, way, depth):
        at = lax.rem(z - depth + 8, 8) if way == 0 else lax.rem(z + depth, 8)
        return 2 * at + (y_hi if group == 0 else 1 - y_hi)

    def far_way(group, k):
        return k % 2 if k in BY_PARTNER else (k + group) % 2

    def a_piece(it, k, slot):
        return a_in.at[it, slot, pl.ds(2 * STARTS[k], 2 * SIZES[k])]

    def z_copy(it, group, k, way, depth):
        piece = a_piece(it, k, z_slot(group, way, depth))
        return remote(piece, piece, sent.at[0], a_recv.at[it, group, k, depth], at_z(1 - 2 * way))

    def a_wait(it, k, depth, recv):
        pieces = a_in.at[it, pl.ds(0, 1 if depth == 4 else 2), pl.ds(2 * STARTS[k], 2 * SIZES[k])]
        remote(pieces, pieces, sent.at[0], recv, mate_hi).wait_recv()

    def y_copy(it, k):
        piece = a_piece(it, k, col)
        return remote(piece, piece, sent.at[0], y_recv.at[it, k], mate_hi)

    def p_copy(it, k, way, depth):
        piece = a_piece(it, k, z_slot(0, way, depth))
        return remote(piece, piece, sent.at[0], p_recv.at[it, BY_PARTNER.index(k), depth - 1], mate_hi)

    def split_a(it, k, slot):
        columns = pl.ds(pl.multiple_of(lax.rem(slot, 2) * 1024 + slot // 2 * TILE, TILE), TILE)
        rows = slice(2 * STARTS[k], 2 * (STARTS[k] + SIZES[k]))
        high, low = halves(a_in[it, slot, rows])
        a_hi[rows, columns] = high
        a_lo[rows, columns] = low

    bufs = {"B": (b_in, b_hi, b_lo), "S": (s_in, s_hi, s_lo)}

    def split_b(it, kind, part, slot):
        buf, high_ref, low_ref = bufs[kind]
        high, low = halves(buf[it, slot, half_of(part), span(part)])
        rows = pl.ds(pl.multiple_of(half_of(part) * 1024 + slot * TILE + STARTS[part] % TILE, 16), SIZES[part])
        high_ref[rows, :] = high
        low_ref[rows, :] = low

    def g_slot(group, step):
        lane = y_lo if group == 0 else 1 - y_lo
        return lane * 4 + lax.rem(x + step + 4, 4)

    def g_copy(it, kind, part, what):
        way = (part + what - 5) % 2
        if part in STRAIGHT[kind]:
            slot = row
            device = (mate_lo, at_x(1), at_x(-1), mate_x(1), mate_x(-1), at_x(2), mate_x(2))[what]
        elif what == 0:
            slot, device = g_slot(0, 0), mate_lo
        elif what < 5:
            slot, device = g_slot((what - 1) // 2, 0), at_x(1 if what % 2 else -1)
        elif what == 6 and kind in FAR_BY_MATE:
            slot, device = g_slot(0, 2), mate_lo
        else:
            slot, device = g_slot(what - 5, 2 * way - 1), at_x(1 - 2 * way)
        piece = bufs[kind][0].at[it, slot, half_of(part), span(part)]
        return remote(piece, piece, sent.at[1 + "BS".index(kind)], g_sem(it, kind, part, what), device)

    def g_sem(it, kind, part, what):
        straight_on = part in STRAIGHT[kind]
        return g_recv.at[it, "BS".index(kind), part, int(what > 2) if straight_on else (0, 1, 1, 2, 2, 3, 4)[what]]

    def g_wait(it, kind, part, what, count):
        pieces = bufs[kind][0].at[it, pl.ds(0, count), half_of(part), span(part)]
        remote(pieces, pieces, sent.at[1 + "BS".index(kind)], g_sem(it, kind, part, what), mate_lo).wait_recv()

    def rows_of(part):
        return pl.ds(STARTS[part], SIZES[part])

    def e_copy(it, part):
        return remote(
            sq_part.at[it, 1 - layer, rows_of(part)], sq_from.at[it, rows_of(part)], sent.at[3], e_recv.at[it, part], sibling
        )

    def pr_copy(it, part):
        rows = pl.ds(part * 256, 256)
        columns = slice(None)
        if it == ITERS - 1:
            columns = pl.ds(pl.multiple_of((1 - layer) * TILE, TILE), TILE)
        return remote(
            pr_part.at[it, rows, columns], pr_from.at[it, rows, columns],
            sent.at[4 + it], e_recv.at[it, PARTS + part], sibling,
        )

    mine = pl.ds(pl.multiple_of(layer * TILE, TILE), TILE)

    def own_part(it, part):
        for side in range(2):
            rows = pl.ds(2 * STARTS[part] + side * SIZES[part], SIZES[part])
            a_in[it, col, rows] = own[half_of(part), side, span(part), mine]
        b_in[it, row, half_of(part), span(part)] = own[half_of(part), layer, span(part)]

    def own_parts(it, half):
        for k in range(PARTS):
            if half_of(k) == half:
                own_part(it, k)

    def iteration(it, update_before):
        def y_begin(k):
            y_copy(it, k).start()

        def z_begin(k):
            z_copy(it, 0, k, 0, 0).start()
            z_copy(it, 0, k, 1, 0).start()
            split_a(it, k, col)

        def y_arrives(k):
            y_copy(it, k).wait_recv()
            if k not in BY_PARTNER:
                z_copy(it, 1, k, 0, 0).start()
                z_copy(it, 1, k, 1, 0).start()
            split_a(it, k, z_slot(1, 0, 0))

        def z_arrives(group, k, depth):
            ways = [way for way in range(2) if depth < 4 or way == far_way(group, k)]
            if group == 1 and k in BY_PARTNER:
                a_wait(it, k, depth, p_recv.at[it, BY_PARTNER.index(k), depth - 1])
            else:
                a_wait(it, k, depth, a_recv.at[it, group, k, depth - 1])
                for way in ways:
                    if depth < 3 or (depth == 3 and way == far_way(group, k)):
                        z_copy(it, group, k, way, depth).start()
                    if k in BY_PARTNER:
                        p_copy(it, k, way, depth).start()
            for way in ways:
                split_a(it, k, z_slot(group, way, depth))

        def column_begin(part):
            for what in range(7 if part in STRAIGHT["B"] else 3):
                g_copy(it, "B", part, what).start()
            split_b(it, "B", part, row)

        def straight(kind, part, far):
            whats = (3, 4, 5, 6) if far else (0, 1, 2)
            g_wait(it, kind, part, whats[0], len(whats))
            slots = (g_slot(1, 0), g_slot(0, -1), g_slot(0, 1), g_slot(1, -1), g_slot(1, 1), g_slot(0, 2), g_slot(1, 2))
            for what in whats:
                split_b(it, kind, part, slots[what])

        def from_mate(kind, part):
            g_wait(it, kind, part, 0, 1)
            g_copy(it, kind, part, 3).start()
            g_copy(it, kind, part, 4).start()
            split_b(it, kind, part, g_slot(1, 0))

        def from_near(kind, part, group):
            g_wait(it, kind, part, 1 + 2 * group, 2)
            for way in range(2):
                if way == (part + group) % 2 and not (group == 1 and kind in FAR_BY_MATE):
                    g_copy(it, kind, part, 5 + group).start()
                split_b(it, kind, part, g_slot(group, 2 * way - 1))

        def from_far(kind, part, group):
            g_wait(it, kind, part, 5 + group, 1)
            if group == 0 and kind in FAR_BY_MATE:
                g_copy(it, kind, part, 6).start()
            split_b(it, kind, part, g_slot(group, 2))

        def square(part):
            rows = slice(2 * STARTS[part], 2 * (STARTS[part] + SIZES[part]))
            value = dot3(a_hi[rows, :], a_lo[rows, :], b_hi[...], b_lo[...])
            sq_part[it, 0, rows_of(part)] = value[: SIZES[part]]
            sq_part[it, 1, rows_of(part)] = value[SIZES[part] :]
            e_copy(it, part).start()

        def square_ready(part):
            e_copy(it, part).wait_recv()
            value = sq_part[it, layer, rows_of(part)] + sq_from[it, rows_of(part)]
            s_in[it, row, half_of(part), span(part)] = tile_mask(filters, (it, 2 * half_of(part) + layer), value)
            for what in range(7 if part in STRAIGHT["S"] else 3):
                g_copy(it, "S", part, what).start()
            split_b(it, "S", part, row)

        def product(first, part):
            rows = slice(part * 256, (part + 1) * 256)
            depth = slice(0, 1024) if first else slice(1024, 2048)
            value = dot3(a_hi[rows, depth], a_lo[rows, depth], s_hi[depth, :], s_lo[depth, :])
            if first:
                pr_part[it, rows, :] = value
            else:
                pr_part[it, rows, :] += value
                pr_copy(it, part).start()

        def update(part):
            pr_copy(it, part).wait_recv()
            for k in range(PARTS):
                for side in range(2):
                    if half_of(k) != part:
                        continue
                    at = 2 * STARTS[k] + side * SIZES[k]
                    rows = slice(at, at + SIZES[k])
                    place = (part, side, span(k))
                    if it < ITERS - 1:
                        value = tile_mask(filters, (it, 2 * part + side), pr_part[it, rows, :] + pr_from[it, rows, :])
                        own[place] = 1.5 * own[place] - 0.5 * value
                    else:
                        value = (pr_part[it, rows, mine] + pr_from[it, rows, mine]) * filters[
                            it, 2 * part + side, layer
                        ].astype(F32)
                        out[place] = 1.5 * own[(*place, mine)] - 0.5 * value

        def own_half(part):
            if update_before is not None:
                update_before(part)
                own_parts(it, part)

        run = {
            "ox": own_half,
            "y": y_begin, "zb": z_begin, "yb": y_arrives, "z": z_arrives, "bg": column_begin, "gm": from_mate,
            "gn": from_near, "gf": from_far, "gd": straight, "sq": square, "sr": square_ready,
            "pr0": lambda part: product(True, part),
        }
        for step in STEPS:
            run[step[0]](*step[1:])
        product(False, 0)
        product(False, 1)
        return update

    parts = [(initial.at[pl.ds(tile * TILE, TILE)], raw.at[tile // 2, tile % 2]) for tile in range(4)]
    parts += [(pattern_in, pattern), (filters_in, filters)]
    fetch = [pltpu.make_async_copy(src, dst, in_sem.at[index]) for index, (src, dst) in enumerate(parts)]
    for copy in fetch:
        copy.start()
    for copy in fetch:
        copy.wait()
    for half in range(2):
        for side in range(2):
            own[half, side] = tile_mask(pattern, (2 * half + side,), raw[half, side])
        own_parts(0, half)
    pl.semaphore_wait(barrier, len(neighbours))
    before = None
    for it in range(ITERS):
        before = iteration(it, before)
    before(0)
    before(1)
    pieces = (a_in.at[:, pl.ds(0, 15)], b_in.at[:, pl.ds(0, 7)], s_in.at[:, pl.ds(0, 7)], sq_from, pr_from.at[0], pr_from.at[1, :, mine])
    for index, piece in enumerate(pieces):
        remote(piece, piece, sent.at[index], in_sem.at[0], sibling).wait_send()


def on_device(initial, pattern, filters):
    dma = pltpu.SemaphoreType.DMA
    vmem = pltpu.VMEM
    out = pl.pallas_call(
        kernel,
        out_shape=jax.ShapeDtypeStruct((2, 2, TILE, TILE), F32),
        in_specs=[
            pl.BlockSpec(memory_space=pltpu.HBM),
            pl.BlockSpec(memory_space=pl.ANY),
            pl.BlockSpec(memory_space=pl.ANY),
        ],
        out_specs=pl.BlockSpec(memory_space=pltpu.VMEM),
        scratch_shapes=[
            vmem((2, 2, TILE, 256), F32),
            pltpu.SMEM((4, 2), jnp.int32),
            pltpu.SMEM((ITERS, 4, 2), jnp.int32),
            vmem((2, 2, TILE, 256), F32),
            vmem((ITERS, 16, 512, TILE), F32),
            vmem((ITERS, 8, 2, TILE, 256), F32),
            vmem((ITERS, 8, 2, TILE, 256), F32),
            vmem((512, 2048), BF16),
            vmem((512, 2048), BF16),
            vmem((2048, 256), BF16),
            vmem((2048, 256), BF16),
            vmem((2048, 256), BF16),
            vmem((2048, 256), BF16),
            vmem((ITERS, 2, 256, 256), F32),
            vmem((ITERS, 256, 256), F32),
            vmem((ITERS, 512, 256), F32),
            vmem((ITERS, 512, 256), F32),
            dma((4 + ITERS,)),
            dma((ITERS, 2, PARTS, 4)),
            dma((ITERS, PARTS)),
            dma((ITERS, max(1, len(BY_PARTNER)), 4)),
            dma((ITERS, 2, PARTS, 5)),
            dma((ITERS, PARTS + 2)),
            dma((6,)),
        ],
        compiler_params=pltpu.CompilerParams(
            collective_id=0, has_side_effects=True, vmem_limit_bytes=54600 << 10
        ),
        name="sign_iterations",
    )(initial, pattern, filters)
    return out.reshape(512, TILE)


def solution(mesh):
    return jax.shard_map(
        on_device,
        mesh=mesh,
        in_specs=(P("row", "col"), P("row", "col"), P(None, "row", "col")),
        out_specs=P("row", ("col", "layer")),
        check_vma=False,
    )
```

```python
import jax
import jax.numpy as jnp
from jax import lax
from jax.experimental import pallas as pl
from jax.experimental.pallas import tpu as pltpu
from jax.sharding import PartitionSpec as P

MESH = pl.DeviceIdType.MESH
TILE = 128
ITERS = 2
SIZES = (64, 64, 64, 32, 32)
PARTS = len(SIZES)
STARTS = tuple(sum(SIZES[:k]) for k in range(PARTS))
F32 = jnp.float32
BF16 = jnp.bfloat16
BY_PARTNER = (1, 3)
FAR_BY_MATE = "S"
STRAIGHT = {"B": (), "S": (4,)}
STEPS = [
    ("ox", 0), ("zb", 0), ("y", 0), ("zb", 1), ("ox", 1), ("bg", 1), ("bg", 0), ("bg", 3), ("zb", 3), ("zb", 2),
    ("y", 2), ("yb", 0), ("z", 0, 0, 1), ("gm", "B", 1), ("bg", 2), ("z", 0, 3, 1), ("z", 0, 1, 1), ("gm", "B", 3),
    ("gn", "B", 0, 0), ("gm", "B", 0), ("yb", 2), ("gn", "B", 1, 0), ("z", 1, 0, 1), ("bg", 4), ("gn", "B", 3, 0),
    ("z", 0, 3, 2), ("z", 0, 0, 2), ("y", 1), ("gm", "B", 2), ("z", 0, 1, 2), ("z", 1, 2, 1), ("gn", "B", 2, 0),
    ("gm", "B", 4), ("gn", "B", 0, 1), ("gn", "B", 4, 0), ("y", 3), ("y", 4), ("z", 1, 0, 2), ("gn", "B", 1, 1),
    ("gf", "B", 3, 0), ("gn", "B", 2, 1), ("z", 0, 2, 1), ("z", 0, 1, 3), ("yb", 1), ("gn", "B", 4, 1),
    ("gn", "B", 3, 1), ("gf", "B", 0, 1), ("z", 0, 0, 3), ("z", 1, 1, 1), ("z", 0, 3, 3), ("z", 1, 0, 3),
    ("zb", 4), ("gf", "B", 0, 0), ("gf", "B", 2, 0), ("gf", "B", 1, 1), ("yb", 4), ("yb", 3), ("gf", "B", 1, 0),
    ("gf", "B", 2, 1), ("z", 1, 2, 2), ("gf", "B", 4, 0), ("gf", "B", 4, 1), ("gf", "B", 3, 1), ("z", 1, 3, 1),
    ("z", 0, 1, 4), ("z", 0, 0, 4), ("z", 0, 2, 2), ("z", 1, 1, 2), ("z", 0, 3, 4), ("z", 1, 1, 3), ("z", 1, 0, 4),
    ("sq", 0), ("z", 1, 3, 2), ("z", 1, 4, 1), ("z", 0, 4, 1), ("z", 1, 1, 4), ("sr", 0), ("sq", 1),
    ("z", 1, 2, 3), ("z", 0, 2, 3), ("sr", 1), ("z", 1, 3, 3), ("z", 1, 3, 4), ("z", 1, 4, 2), ("sq", 3),
    ("gm", "S", 0), ("z", 0, 4, 2), ("gn", "S", 0, 0), ("sr", 3), ("z", 1, 2, 4), ("z", 0, 2, 4), ("sq", 2),
    ("gn", "S", 1, 0), ("z", 1, 4, 3), ("sr", 2), ("z", 0, 4, 3), ("gf", "S", 0, 0), ("gm", "S", 3),
    ("gm", "S", 1), ("gn", "S", 3, 0), ("z", 1, 4, 4), ("z", 0, 4, 4), ("sq", 4), ("gf", "S", 1, 0),
    ("gn", "S", 2, 0), ("sr", 4), ("gn", "S", 1, 1), ("gf", "S", 1, 1), ("gn", "S", 0, 1), ("gn", "S", 3, 1),
    ("gf", "S", 3, 0), ("gf", "S", 0, 1), ("gm", "S", 2), ("gf", "S", 2, 0), ("gd", "S", 4, 0), ("pr0", 1),
    ("pr0", 0), ("gf", "S", 3, 1), ("gd", "S", 4, 1), ("gn", "S", 2, 1), ("gf", "S", 2, 1),
]


def halves(value):
    high = value.astype(BF16)
    return high, (value - high.astype(F32)).astype(BF16)


def dot3(a_high, a_low, b_high, b_low):
    def dot(a, b):
        return jnp.dot(a, b, preferred_element_type=F32)

    return dot(a_high, b_high) + (dot(a_high, b_low) + dot(a_low, b_high))


def kernel(
    initial, pattern_in, filters_in, out,
    raw, pattern, filters, own, a_in, b_in, s_in, a_hi, a_lo, b_hi, b_lo, s_hi, s_lo, sq_part, sq_from, pr_part, pr_from,
    sent, a_recv, y_recv, p_recv, g_recv, e_recv, in_sem,
):
    row, col, layer = lax.axis_index("row"), lax.axis_index("col"), lax.axis_index("layer")
    x, y_lo = lax.rem(row, 4), row // 4
    z, y_hi = col // 2, lax.rem(col, 2)
    def at_x(step):
        return {"row": y_lo * 4 + lax.rem(x + step + 4, 4)}

    def at_z(step):
        return {"col": lax.rem(z + step + 8, 8) * 2 + y_hi}

    def mate_x(step):
        return {"row": (1 - y_lo) * 4 + lax.rem(x + step + 4, 4)}

    mate_lo = mate_x(0)
    mate_hi = {"col": z * 2 + (1 - y_hi)}
    sibling = {"layer": 1 - layer}

    barrier = pltpu.get_barrier_semaphore()
    neighbours = (at_x(1), at_x(-1), at_z(1), at_z(-1), mate_lo, mate_hi, sibling)
    if any(STRAIGHT.values()):
        neighbours += (at_x(2), mate_x(1), mate_x(-1), mate_x(2))
    for device in neighbours:
        pl.semaphore_signal(barrier, inc=1, device_id=device, device_id_type=MESH)

    def half_of(k):
        return STARTS[k] // TILE

    def span(k):
        return pl.ds(STARTS[k] % TILE, SIZES[k])

    def tile_mask(ref, index, value):
        parts = []
        for ct in range(2):
            parts.append(value[:, ct * TILE : (ct + 1) * TILE] * ref[(*index[:-1], ct, index[-1])].astype(F32))
        return jnp.concatenate(parts, axis=1)

    def remote(src, dst, send, recv, device):
        return pltpu.make_async_remote_copy(
            src_ref=src, dst_ref=dst, send_sem=send, recv_sem=recv, device_id=device, device_id_type=MESH
        )

    def z_slot(group, way, depth):
        at = lax.rem(z - depth + 8, 8) if way == 0 else lax.rem(z + depth, 8)
        return 2 * at + (y_hi if group == 0 else 1 - y_hi)

    def far_way(group, k):
        return k % 2 if k in BY_PARTNER else (k + group) % 2

    def a_piece(it, k, slot):
        return a_in.at[it, slot, pl.ds(2 * STARTS[k], 2 * SIZES[k])]

    def z_copy(it, group, k, way, depth):
        piece = a_piece(it, k, z_slot(group, way, depth))
        return remote(piece, piece, sent.at[0], a_recv.at[it, group, k, depth], at_z(1 - 2 * way))

    def a_wait(it, k, depth, recv):
        pieces = a_in.at[it, pl.ds(0, 1 if depth == 4 else 2), pl.ds(2 * STARTS[k], 2 * SIZES[k])]
        remote(pieces, pieces, sent.at[0], recv, mate_hi).wait_recv()

    def y_copy(it, k):
        piece = a_piece(it, k, col)
        return remote(piece, piece, sent.at[0], y_recv.at[it, k], mate_hi)

    def p_copy(it, k, way, depth):
        piece = a_piece(it, k, z_slot(0, way, depth))
        return remote(piece, piece, sent.at[0], p_recv.at[it, BY_PARTNER.index(k), depth - 1], mate_hi)

    def split_a(it, k, slot):
        columns = pl.ds(pl.multiple_of(lax.rem(slot, 2) * 1024 + slot // 2 * TILE, TILE), TILE)
        rows = slice(2 * STARTS[k], 2 * (STARTS[k] + SIZES[k]))
        high, low = halves(a_in[it, slot, rows])
        a_hi[rows, columns] = high
        a_lo[rows, columns] = low

    bufs = {"B": (b_in, b_hi, b_lo), "S": (s_in, s_hi, s_lo)}

    def split_b(it, kind, part, slot):
        buf, high_ref, low_ref = bufs[kind]
        high, low = halves(buf[it, slot, half_of(part), span(part)])
        rows = pl.ds(pl.multiple_of(half_of(part) * 1024 + slot * TILE + STARTS[part] % TILE, 16), SIZES[part])
        high_ref[rows, :] = high
        low_ref[rows, :] = low

    def g_slot(group, step):
        lane = y_lo if group == 0 else 1 - y_lo
        return lane * 4 + lax.rem(x + step + 4, 4)

    def g_copy(it, kind, part, what):
        way = (part + what - 5) % 2
        if part in STRAIGHT[kind]:
            slot = row
            device = (mate_lo, at_x(1), at_x(-1), mate_x(1), mate_x(-1), at_x(2), mate_x(2))[what]
        elif what == 0:
            slot, device = g_slot(0, 0), mate_lo
        elif what < 5:
            slot, device = g_slot((what - 1) // 2, 0), at_x(1 if what % 2 else -1)
        elif what == 6 and kind in FAR_BY_MATE:
            slot, device = g_slot(0, 2), mate_lo
        else:
            slot, device = g_slot(what - 5, 2 * way - 1), at_x(1 - 2 * way)
        piece = bufs[kind][0].at[it, slot, half_of(part), span(part)]
        return remote(piece, piece, sent.at[1 + "BS".index(kind)], g_sem(it, kind, part, what), device)

    def g_sem(it, kind, part, what):
        straight_on = part in STRAIGHT[kind]
        return g_recv.at[it, "BS".index(kind), part, int(what > 2) if straight_on else (0, 1, 1, 2, 2, 3, 4)[what]]

    def g_wait(it, kind, part, what, count):
        pieces = bufs[kind][0].at[it, pl.ds(0, count), half_of(part), span(part)]
        remote(pieces, pieces, sent.at[1 + "BS".index(kind)], g_sem(it, kind, part, what), mate_lo).wait_recv()

    def rows_of(part):
        return pl.ds(STARTS[part], SIZES[part])

    def e_copy(it, part):
        return remote(
            sq_part.at[it, 1 - layer, rows_of(part)], sq_from.at[it, rows_of(part)], sent.at[3], e_recv.at[it, part], sibling
        )

    def pr_copy(it, part):
        rows = pl.ds(part * 256, 256)
        columns = slice(None)
        if it == ITERS - 1:
            columns = pl.ds(pl.multiple_of((1 - layer) * TILE, TILE), TILE)
        return remote(
            pr_part.at[it, rows, columns], pr_from.at[it, rows, columns],
            sent.at[4 + it], e_recv.at[it, PARTS + part], sibling,
        )

    mine = pl.ds(pl.multiple_of(layer * TILE, TILE), TILE)

    def own_part(it, part):
        for side in range(2):
            rows = pl.ds(2 * STARTS[part] + side * SIZES[part], SIZES[part])
            a_in[it, col, rows] = own[half_of(part), side, span(part), mine]
        b_in[it, row, half_of(part), span(part)] = own[half_of(part), layer, span(part)]

    def own_parts(it, half):
        for k in range(PARTS):
            if half_of(k) == half:
                own_part(it, k)

    def iteration(it, update_before):
        def y_begin(k):
            y_copy(it, k).start()

        def z_begin(k):
            z_copy(it, 0, k, 0, 0).start()
            z_copy(it, 0, k, 1, 0).start()
            split_a(it, k, col)

        def y_arrives(k):
            y_copy(it, k).wait_recv()
            if k not in BY_PARTNER:
                z_copy(it, 1, k, 0, 0).start()
                z_copy(it, 1, k, 1, 0).start()
            split_a(it, k, z_slot(1, 0, 0))

        def z_arrives(group, k, depth):
            ways = [way for way in range(2) if depth < 4 or way == far_way(group, k)]
            if group == 1 and k in BY_PARTNER:
                a_wait(it, k, depth, p_recv.at[it, BY_PARTNER.index(k), depth - 1])
            else:
                a_wait(it, k, depth, a_recv.at[it, group, k, depth - 1])
                for way in ways:
                    if depth < 3 or (depth == 3 and way == far_way(group, k)):
                        z_copy(it, group, k, way, depth).start()
                    if k in BY_PARTNER:
                        p_copy(it, k, way, depth).start()
            for way in ways:
                split_a(it, k, z_slot(group, way, depth))

        def column_begin(part):
            for what in range(7 if part in STRAIGHT["B"] else 3):
                g_copy(it, "B", part, what).start()
            split_b(it, "B", part, row)

        def straight(kind, part, far):
            whats = (3, 4, 5, 6) if far else (0, 1, 2)
            g_wait(it, kind, part, whats[0], len(whats))
            slots = (g_slot(1, 0), g_slot(0, -1), g_slot(0, 1), g_slot(1, -1), g_slot(1, 1), g_slot(0, 2), g_slot(1, 2))
            for what in whats:
                split_b(it, kind, part, slots[what])

        def from_mate(kind, part):
            g_wait(it, kind, part, 0, 1)
            g_copy(it, kind, part, 3).start()
            g_copy(it, kind, part, 4).start()
            split_b(it, kind, part, g_slot(1, 0))

        def from_near(kind, part, group):
            g_wait(it, kind, part, 1 + 2 * group, 2)
            for way in range(2):
                if way == (part + group) % 2 and not (group == 1 and kind in FAR_BY_MATE):
                    g_copy(it, kind, part, 5 + group).start()
                split_b(it, kind, part, g_slot(group, 2 * way - 1))

        def from_far(kind, part, group):
            g_wait(it, kind, part, 5 + group, 1)
            if group == 0 and kind in FAR_BY_MATE:
                g_copy(it, kind, part, 6).start()
            split_b(it, kind, part, g_slot(group, 2))

        def square(part):
            rows = slice(2 * STARTS[part], 2 * (STARTS[part] + SIZES[part]))
            value = dot3(a_hi[rows, :], a_lo[rows, :], b_hi[...], b_lo[...])
            sq_part[it, 0, rows_of(part)] = value[: SIZES[part]]
            sq_part[it, 1, rows_of(part)] = value[SIZES[part] :]
            e_copy(it, part).start()

        def square_ready(part):
            e_copy(it, part).wait_recv()
            value = sq_part[it, layer, rows_of(part)] + sq_from[it, rows_of(part)]
            s_in[it, row, half_of(part), span(part)] = tile_mask(filters, (it, 2 * half_of(part) + layer), value)
            for what in range(7 if part in STRAIGHT["S"] else 3):
                g_copy(it, "S", part, what).start()
            split_b(it, "S", part, row)

        def product(first, part):
            rows = slice(part * 256, (part + 1) * 256)
            depth = slice(0, 1024) if first else slice(1024, 2048)
            value = dot3(a_hi[rows, depth], a_lo[rows, depth], s_hi[depth, :], s_lo[depth, :])
            if first:
                pr_part[it, rows, :] = value
            else:
                pr_part[it, rows, :] += value
                pr_copy(it, part).start()

        def update(part):
            pr_copy(it, part).wait_recv()
            for k in range(PARTS):
                for side in range(2):
                    if half_of(k) != part:
                        continue
                    at = 2 * STARTS[k] + side * SIZES[k]
                    rows = slice(at, at + SIZES[k])
                    place = (part, side, span(k))
                    if it < ITERS - 1:
                        value = tile_mask(filters, (it, 2 * part + side), pr_part[it, rows, :] + pr_from[it, rows, :])
                        own[place] = 1.5 * own[place] - 0.5 * value
                    else:
                        value = (pr_part[it, rows, mine] + pr_from[it, rows, mine]) * filters[
                            it, layer, 2 * part + side
                        ].astype(F32)
                        out[place] = 1.5 * own[(*place, mine)] - 0.5 * value

        def own_half(part):
            if update_before is not None:
                update_before(part)
                own_parts(it, part)

        run = {
            "ox": own_half,
            "y": y_begin, "zb": z_begin, "yb": y_arrives, "z": z_arrives, "bg": column_begin, "gm": from_mate,
            "gn": from_near, "gf": from_far, "gd": straight, "sq": square, "sr": square_ready,
            "pr0": lambda part: product(True, part),
        }
        for step in STEPS:
            run[step[0]](*step[1:])
        product(False, 0)
        product(False, 1)
        return update

    parts = [(initial.at[pl.ds(tile * TILE, TILE)], raw.at[tile // 2, tile % 2]) for tile in range(4)]
    parts += [(pattern_in, pattern), (filters_in, filters)]
    fetch = [pltpu.make_async_copy(src, dst, in_sem.at[index]) for index, (src, dst) in enumerate(parts)]
    for copy in fetch:
        copy.start()
    for copy in fetch:
        copy.wait()
    for half in range(2):
        for side in range(2):
            own[half, side] = tile_mask(pattern, (2 * half + side,), raw[half, side])
        own_parts(0, half)
    pl.semaphore_wait(barrier, len(neighbours))
    before = None
    for it in range(ITERS):
        before = iteration(it, before)
    before(0)
    before(1)
    pieces = (a_in.at[:, pl.ds(0, 15)], b_in.at[:, pl.ds(0, 7)], s_in.at[:, pl.ds(0, 7)], sq_from, pr_from.at[0], pr_from.at[1, :, mine])
    for index, piece in enumerate(pieces):
        remote(piece, piece, sent.at[index], in_sem.at[0], sibling).wait_send()


def on_device(initial, pattern, filters):
    dma = pltpu.SemaphoreType.DMA
    vmem = pltpu.VMEM
    out = pl.pallas_call(
        kernel,
        out_shape=jax.ShapeDtypeStruct((2, 2, TILE, TILE), F32),
        in_specs=[
            pl.BlockSpec(memory_space=pltpu.HBM),
            pl.BlockSpec(memory_space=pl.ANY),
            pl.BlockSpec(memory_space=pl.ANY),
        ],
        out_specs=pl.BlockSpec(memory_space=pltpu.VMEM),
        scratch_shapes=[
            vmem((2, 2, TILE, 256), F32),
            pltpu.SMEM((2, 4), jnp.int32),
            pltpu.SMEM((ITERS, 2, 4), jnp.int32),
            vmem((2, 2, TILE, 256), F32),
            vmem((ITERS, 16, 512, TILE), F32),
            vmem((ITERS, 8, 2, TILE, 256), F32),
            vmem((ITERS, 8, 2, TILE, 256), F32),
            vmem((512, 2048), BF16),
            vmem((512, 2048), BF16),
            vmem((2048, 256), BF16),
            vmem((2048, 256), BF16),
            vmem((2048, 256), BF16),
            vmem((2048, 256), BF16),
            vmem((ITERS, 2, 256, 256), F32),
            vmem((ITERS, 256, 256), F32),
            vmem((ITERS, 512, 256), F32),
            vmem((ITERS, 512, 256), F32),
            dma((4 + ITERS,)),
            dma((ITERS, 2, PARTS, 4)),
            dma((ITERS, PARTS)),
            dma((ITERS, max(1, len(BY_PARTNER)), 4)),
            dma((ITERS, 2, PARTS, 5)),
            dma((ITERS, PARTS + 2)),
            dma((6,)),
        ],
        compiler_params=pltpu.CompilerParams(
            collective_id=0, has_side_effects=True, vmem_limit_bytes=54600 << 10
        ),
        name="sign_iterations",
    )(initial, pattern.T, filters.swapaxes(1, 2))
    return out.reshape(512, TILE)


def solution(mesh):
    return jax.shard_map(
        on_device,
        mesh=mesh,
        in_specs=(P("row", "col"), P("row", "col"), P(None, "row", "col")),
        out_specs=P("row", ("col", "layer")),
        check_vma=False,
    )
```

```python
import jax
import jax.numpy as jnp
from jax import lax
from jax.experimental import pallas as pl
from jax.experimental.pallas import tpu as pltpu
from jax.sharding import PartitionSpec as P

MESH = pl.DeviceIdType.MESH
TILE = 128
ITERS = 2
SIZES = (64, 64, 64, 32, 32)
PARTS = len(SIZES)
STARTS = tuple(sum(SIZES[:k]) for k in range(PARTS))
F32 = jnp.float32
BF16 = jnp.bfloat16
BY_PARTNER = (1, 3)
FAR_BY_MATE = "S"
STRAIGHT = {"B": (), "S": (4,)}
STEPS = [
    ("ox", 0), ("zb", 0), ("y", 0), ("zb", 1), ("ox", 1), ("bg", 1), ("bg", 0), ("bg", 3), ("zb", 3), ("zb", 2),
    ("y", 2), ("yb", 0), ("z", 0, 0, 1), ("gm", "B", 1), ("bg", 2), ("z", 0, 3, 1), ("z", 0, 1, 1), ("gm", "B", 3),
    ("gn", "B", 0, 0), ("gm", "B", 0), ("yb", 2), ("gn", "B", 1, 0), ("z", 1, 0, 1), ("bg", 4), ("gn", "B", 3, 0),
    ("z", 0, 3, 2), ("z", 0, 0, 2), ("y", 1), ("gm", "B", 2), ("z", 0, 1, 2), ("z", 1, 2, 1), ("gn", "B", 2, 0),
    ("gm", "B", 4), ("gn", "B", 0, 1), ("gn", "B", 4, 0), ("y", 3), ("y", 4), ("z", 1, 0, 2), ("gn", "B", 1, 1),
    ("gf", "B", 3, 0), ("gn", "B", 2, 1), ("z", 0, 2, 1), ("z", 0, 1, 3), ("yb", 1), ("gn", "B", 4, 1),
    ("gn", "B", 3, 1), ("gf", "B", 0, 1), ("z", 0, 0, 3), ("z", 1, 1, 1), ("z", 0, 3, 3), ("z", 1, 0, 3),
    ("zb", 4), ("gf", "B", 0, 0), ("gf", "B", 2, 0), ("gf", "B", 1, 1), ("yb", 4), ("yb", 3), ("gf", "B", 1, 0),
    ("gf", "B", 2, 1), ("z", 1, 2, 2), ("gf", "B", 4, 0), ("gf", "B", 4, 1), ("gf", "B", 3, 1), ("z", 1, 3, 1),
    ("z", 0, 1, 4), ("z", 0, 0, 4), ("z", 0, 2, 2), ("z", 1, 1, 2), ("z", 0, 3, 4), ("z", 1, 1, 3), ("z", 1, 0, 4),
    ("sq", 0), ("z", 1, 3, 2), ("z", 1, 4, 1), ("z", 0, 4, 1), ("z", 1, 1, 4), ("sr", 0), ("sq", 1),
    ("z", 1, 2, 3), ("z", 0, 2, 3), ("sr", 1), ("z", 1, 3, 3), ("z", 1, 3, 4), ("z", 1, 4, 2), ("sq", 3),
    ("gm", "S", 0), ("z", 0, 4, 2), ("gn", "S", 0, 0), ("sr", 3), ("z", 1, 2, 4), ("z", 0, 2, 4), ("sq", 2),
    ("gn", "S", 1, 0), ("z", 1, 4, 3), ("sr", 2), ("z", 0, 4, 3), ("gf", "S", 0, 0), ("gm", "S", 3),
    ("gm", "S", 1), ("gn", "S", 3, 0), ("z", 1, 4, 4), ("z", 0, 4, 4), ("sq", 4), ("gf", "S", 1, 0),
    ("gn", "S", 2, 0), ("sr", 4), ("gn", "S", 1, 1), ("gf", "S", 1, 1), ("gn", "S", 0, 1), ("gn", "S", 3, 1),
    ("gf", "S", 3, 0), ("gf", "S", 0, 1), ("gm", "S", 2), ("gf", "S", 2, 0), ("gd", "S", 4, 0), ("pr0", 1),
    ("pr0", 0), ("gf", "S", 3, 1), ("gd", "S", 4, 1), ("gn", "S", 2, 1), ("gf", "S", 2, 1),
]


def halves(value):
    high = value.astype(BF16)
    return high, (value - high.astype(F32)).astype(BF16)


def dot3(a_high, a_low, b_high, b_low):
    def dot(a, b):
        return jnp.dot(a, b, preferred_element_type=F32)

    return dot(a_high, b_high) + (dot(a_high, b_low) + dot(a_low, b_high))


def kernel(
    initial, pattern_in, filters_in, out,
    raw, pattern, filters, own, a_in, b_in, s_in, a_hi, a_lo, b_hi, b_lo, s_hi, s_lo, sq_part, sq_from, pr_part, pr_from,
    sent, a_recv, y_recv, g_recv, e_recv, in_sem,
):
    row, col, layer = lax.axis_index("row"), lax.axis_index("col"), lax.axis_index("layer")
    x, y_lo = lax.rem(row, 4), row // 4
    z, y_hi = col // 2, lax.rem(col, 2)
    def at_x(step):
        return {"row": y_lo * 4 + lax.rem(x + step + 4, 4)}

    def at_z(step):
        return {"col": lax.rem(z + step + 8, 8) * 2 + y_hi}

    def mate_x(step):
        return {"row": (1 - y_lo) * 4 + lax.rem(x + step + 4, 4)}

    mate_lo = mate_x(0)
    mate_hi = {"col": z * 2 + (1 - y_hi)}
    sibling = {"layer": 1 - layer}

    barrier = pltpu.get_barrier_semaphore()
    neighbours = (at_x(1), at_x(-1), at_z(1), at_z(-1), mate_lo, mate_hi, sibling)
    if any(STRAIGHT.values()):
        neighbours += (at_x(2), mate_x(1), mate_x(-1), mate_x(2))
    for device in neighbours:
        pl.semaphore_signal(barrier, inc=1, device_id=device, device_id_type=MESH)

    def half_of(k):
        return STARTS[k] // TILE

    def span(k):
        return pl.ds(STARTS[k] % TILE, SIZES[k])

    def tile_mask(ref, index, value):
        parts = []
        for ct in range(2):
            parts.append(value[:, ct * TILE : (ct + 1) * TILE] * ref[(*index[:-1], ct, index[-1])].astype(F32))
        return jnp.concatenate(parts, axis=1)

    def remote(src, dst, send, recv, device):
        return pltpu.make_async_remote_copy(
            src_ref=src, dst_ref=dst, send_sem=send, recv_sem=recv, device_id=device, device_id_type=MESH
        )

    def z_slot(group, way, depth):
        at = lax.rem(z - depth + 8, 8) if way == 0 else lax.rem(z + depth, 8)
        return 2 * at + (y_hi if group == 0 else 1 - y_hi)

    def far_way(group, k):
        return k % 2 if k in BY_PARTNER else (k + group) % 2

    def a_piece(it, k, slot):
        return a_in.at[it, slot, pl.ds(2 * STARTS[k], 2 * SIZES[k])]

    def z_copy(it, group, k, way, depth):
        piece = a_piece(it, k, z_slot(group, way, depth))
        return remote(piece, piece, sent.at[0], a_recv.at[it, group, k, depth], at_z(1 - 2 * way))

    def a_wait(it, k, depth, recv):
        pieces = a_in.at[it, pl.ds(0, 1 if depth == 4 else 2), pl.ds(2 * STARTS[k], 2 * SIZES[k])]
        remote(pieces, pieces, sent.at[0], recv, mate_hi).wait_recv()

    def y_copy(it, k):
        piece = a_piece(it, k, col)
        return remote(piece, piece, sent.at[0], y_recv.at[it, k], mate_hi)

    def p_copy(it, k, way, depth):
        piece = a_piece(it, k, z_slot(0, way, depth))
        return remote(piece, piece, sent.at[0], a_recv.at[it, 1, k, depth - 1], mate_hi)

    def split_a(it, k, slot):
        columns = pl.ds(pl.multiple_of(lax.rem(slot, 2) * 1024 + slot // 2 * TILE, TILE), TILE)
        rows = slice(2 * STARTS[k], 2 * (STARTS[k] + SIZES[k]))
        high, low = halves(a_in[it, slot, rows])
        a_hi[rows, columns] = high
        a_lo[rows, columns] = low

    bufs = {"B": (b_in, b_hi, b_lo), "S": (s_in, s_hi, s_lo)}

    def split_b(it, kind, part, slot):
        buf, high_ref, low_ref = bufs[kind]
        high, low = halves(buf[it, slot, half_of(part), span(part)])
        rows = pl.ds(pl.multiple_of(half_of(part) * 1024 + slot * TILE + STARTS[part] % TILE, 16), SIZES[part])
        high_ref[rows, :] = high
        low_ref[rows, :] = low

    def g_slot(group, step):
        lane = y_lo if group == 0 else 1 - y_lo
        return lane * 4 + lax.rem(x + step + 4, 4)

    def g_copy(it, kind, part, what):
        way = (part + what - 5) % 2
        if part in STRAIGHT[kind]:
            slot = row
            device = (mate_lo, at_x(1), at_x(-1), mate_x(1), mate_x(-1), at_x(2), mate_x(2))[what]
        elif what == 0:
            slot, device = g_slot(0, 0), mate_lo
        elif what < 5:
            slot, device = g_slot((what - 1) // 2, 0), at_x(1 if what % 2 else -1)
        elif what == 6 and kind in FAR_BY_MATE:
            slot, device = g_slot(0, 2), mate_lo
        else:
            slot, device = g_slot(what - 5, 2 * way - 1), at_x(1 - 2 * way)
        piece = bufs[kind][0].at[it, slot, half_of(part), span(part)]
        return remote(piece, piece, sent.at[1 + "BS".index(kind)], g_sem(it, kind, part, what), device)

    def g_sem(it, kind, part, what):
        straight_on = part in STRAIGHT[kind]
        return g_recv.at[it, "BS".index(kind), part, int(what > 2) if straight_on else (0, 1, 1, 2, 2, 3, 4)[what]]

    def g_wait(it, kind, part, what, count):
        pieces = bufs[kind][0].at[it, pl.ds(0, count), half_of(part), span(part)]
        remote(pieces, pieces, sent.at[1 + "BS".index(kind)], g_sem(it, kind, part, what), mate_lo).wait_recv()

    def rows_of(part):
        return pl.ds(STARTS[part], SIZES[part])

    def e_copy(it, part):
        return remote(
            sq_part.at[it, 1 - layer, rows_of(part)], sq_from.at[it, rows_of(part)], sent.at[3], e_recv.at[it, part], sibling
        )

    def pr_copy(it, part):
        rows = pl.ds(part * 256, 256)
        columns = slice(None)
        if it == ITERS - 1:
            columns = pl.ds(pl.multiple_of((1 - layer) * TILE, TILE), TILE)
        return remote(
            pr_part.at[it, rows, columns], pr_from.at[it, rows, columns],
            sent.at[4 + it], e_recv.at[it, PARTS + part], sibling,
        )

    mine = pl.ds(pl.multiple_of(layer * TILE, TILE), TILE)

    def own_part(it, part):
        for side in range(2):
            rows = pl.ds(2 * STARTS[part] + side * SIZES[part], SIZES[part])
            a_in[it, col, rows] = own[half_of(part), side, span(part), mine]
        b_in[it, row, half_of(part), span(part)] = own[half_of(part), layer, span(part)]

    def own_parts(it, half):
        for k in range(PARTS):
            if half_of(k) == half:
                own_part(it, k)

    def iteration(it, update_before):
        def y_begin(k):
            y_copy(it, k).start()

        def z_begin(k):
            z_copy(it, 0, k, 0, 0).start()
            z_copy(it, 0, k, 1, 0).start()
            split_a(it, k, col)

        def y_arrives(k):
            y_copy(it, k).wait_recv()
            if k not in BY_PARTNER:
                z_copy(it, 1, k, 0, 0).start()
                z_copy(it, 1, k, 1, 0).start()
            split_a(it, k, z_slot(1, 0, 0))

        def z_arrives(group, k, depth):
            ways = [way for way in range(2) if depth < 4 or way == far_way(group, k)]
            if group == 1 and k in BY_PARTNER:
                a_wait(it, k, depth, a_recv.at[it, 1, k, depth - 1])
            else:
                a_wait(it, k, depth, a_recv.at[it, group, k, depth - 1])
                for way in ways:
                    if depth < 3 or (depth == 3 and way == far_way(group, k)):
                        z_copy(it, group, k, way, depth).start()
                    if k in BY_PARTNER:
                        p_copy(it, k, way, depth).start()
            for way in ways:
                split_a(it, k, z_slot(group, way, depth))

        def column_begin(part):
            for what in range(7 if part in STRAIGHT["B"] else 3):
                g_copy(it, "B", part, what).start()
            split_b(it, "B", part, row)

        def straight(kind, part, far):
            whats = (3, 4, 5, 6) if far else (0, 1, 2)
            g_wait(it, kind, part, whats[0], len(whats))
            slots = (g_slot(1, 0), g_slot(0, -1), g_slot(0, 1), g_slot(1, -1), g_slot(1, 1), g_slot(0, 2), g_slot(1, 2))
            for what in whats:
                split_b(it, kind, part, slots[what])

        def from_mate(kind, part):
            g_wait(it, kind, part, 0, 1)
            g_copy(it, kind, part, 3).start()
            g_copy(it, kind, part, 4).start()
            split_b(it, kind, part, g_slot(1, 0))

        def from_near(kind, part, group):
            g_wait(it, kind, part, 1 + 2 * group, 2)
            for way in range(2):
                if way == (part + group) % 2 and not (group == 1 and kind in FAR_BY_MATE):
                    g_copy(it, kind, part, 5 + group).start()
                split_b(it, kind, part, g_slot(group, 2 * way - 1))

        def from_far(kind, part, group):
            g_wait(it, kind, part, 5 + group, 1)
            if group == 0 and kind in FAR_BY_MATE:
                g_copy(it, kind, part, 6).start()
            split_b(it, kind, part, g_slot(group, 2))

        def square(part):
            rows = slice(2 * STARTS[part], 2 * (STARTS[part] + SIZES[part]))
            value = dot3(a_hi[rows, :], a_lo[rows, :], b_hi[...], b_lo[...])
            sq_part[it, 0, rows_of(part)] = value[: SIZES[part]]
            sq_part[it, 1, rows_of(part)] = value[SIZES[part] :]
            e_copy(it, part).start()

        def square_ready(part):
            e_copy(it, part).wait_recv()
            value = sq_part[it, layer, rows_of(part)] + sq_from[it, rows_of(part)]
            s_in[it, row, half_of(part), span(part)] = tile_mask(filters, (it, 2 * half_of(part) + layer), value)
            for what in range(7 if part in STRAIGHT["S"] else 3):
                g_copy(it, "S", part, what).start()
            split_b(it, "S", part, row)

        def product(first, part):
            rows = slice(part * 256, (part + 1) * 256)
            depth = slice(0, 1024) if first else slice(1024, 2048)
            value = dot3(a_hi[rows, depth], a_lo[rows, depth], s_hi[depth, :], s_lo[depth, :])
            if first:
                pr_part[it, rows, :] = value
            else:
                pr_part[it, rows, :] += value
                pr_copy(it, part).start()

        def update(part):
            pr_copy(it, part).wait_recv()
            for k in range(PARTS):
                for side in range(2):
                    if half_of(k) != part:
                        continue
                    at = 2 * STARTS[k] + side * SIZES[k]
                    rows = slice(at, at + SIZES[k])
                    place = (part, side, span(k))
                    if it < ITERS - 1:
                        value = tile_mask(filters, (it, 2 * part + side), pr_part[it, rows, :] + pr_from[it, rows, :])
                        own[place] = 1.5 * own[place] - 0.5 * value
                    else:
                        value = (pr_part[it, rows, mine] + pr_from[it, rows, mine]) * filters[
                            it, layer, 2 * part + side
                        ].astype(F32)
                        out[place] = 1.5 * own[(*place, mine)] - 0.5 * value

        def own_half(part):
            if update_before is not None:
                update_before(part)
                own_parts(it, part)

        run = {
            "ox": own_half,
            "y": y_begin, "zb": z_begin, "yb": y_arrives, "z": z_arrives, "bg": column_begin, "gm": from_mate,
            "gn": from_near, "gf": from_far, "gd": straight, "sq": square, "sr": square_ready,
            "pr0": lambda part: product(True, part),
        }
        for step in STEPS:
            run[step[0]](*step[1:])
        product(False, 0)
        product(False, 1)
        return update

    parts = [(initial.at[pl.ds(tile * TILE, TILE)], raw.at[tile // 2, tile % 2]) for tile in range(4)]
    parts += [(pattern_in, pattern), (filters_in, filters)]
    fetch = [pltpu.make_async_copy(src, dst, in_sem.at[index]) for index, (src, dst) in enumerate(parts)]
    for copy in fetch:
        copy.start()
    for copy in fetch:
        copy.wait()
    for half in range(2):
        for side in range(2):
            own[half, side] = tile_mask(pattern, (2 * half + side,), raw[half, side])
        own_parts(0, half)
    pl.semaphore_wait(barrier, len(neighbours))
    before = None
    for it in range(ITERS):
        before = iteration(it, before)
    before(0)
    before(1)
    pieces = (a_in.at[:, pl.ds(0, 15)], b_in.at[:, pl.ds(0, 7)], s_in.at[:, pl.ds(0, 7)], sq_from, pr_from.at[0], pr_from.at[1, :, mine])
    for index, piece in enumerate(pieces):
        remote(piece, piece, sent.at[index], in_sem.at[0], sibling).wait_send()


def on_device(initial, pattern, filters):
    dma = pltpu.SemaphoreType.DMA
    vmem = pltpu.VMEM
    out = pl.pallas_call(
        kernel,
        out_shape=jax.ShapeDtypeStruct((2, 2, TILE, TILE), F32),
        in_specs=[
            pl.BlockSpec(memory_space=pltpu.HBM),
            pl.BlockSpec(memory_space=pl.ANY),
            pl.BlockSpec(memory_space=pl.ANY),
        ],
        out_specs=pl.BlockSpec(memory_space=pltpu.VMEM),
        scratch_shapes=[
            vmem((2, 2, TILE, 256), F32),
            pltpu.SMEM((2, 4), jnp.int32),
            pltpu.SMEM((ITERS, 2, 4), jnp.int32),
            vmem((2, 2, TILE, 256), F32),
            vmem((ITERS, 16, 512, TILE), F32),
            vmem((ITERS, 8, 2, TILE, 256), F32),
            vmem((ITERS, 8, 2, TILE, 256), F32),
            vmem((512, 2048), BF16),
            vmem((512, 2048), BF16),
            vmem((2048, 256), BF16),
            vmem((2048, 256), BF16),
            vmem((2048, 256), BF16),
            vmem((2048, 256), BF16),
            vmem((ITERS, 2, 256, 256), F32),
            vmem((ITERS, 256, 256), F32),
            vmem((ITERS, 512, 256), F32),
            vmem((ITERS, 512, 256), F32),
            dma((4 + ITERS,)),
            dma((ITERS, 2, PARTS, 4)),
            dma((ITERS, PARTS)),
            dma((ITERS, 2, PARTS, 5)),
            dma((ITERS, PARTS + 2)),
            dma((6,)),
        ],
        compiler_params=pltpu.CompilerParams(
            collective_id=0, has_side_effects=True, vmem_limit_bytes=54600 << 10
        ),
        name="sign_iterations",
    )(initial, pattern.T, filters.swapaxes(1, 2))
    return out.reshape(512, TILE)


def solution(mesh):
    return jax.shard_map(
        on_device,
        mesh=mesh,
        in_specs=(P("row", "col"), P("row", "col"), P(None, "row", "col")),
        out_specs=P("row", ("col", "layer")),
        check_vma=False,
    )
```
